32 devices in a mesh: rows: 8 (over z, y), heads: 4 (over x, core).
Axes of the slice: x: 2, y: 2, z: 4, core: 2. Of those that a mesh axis runs over, the one named last changes fastest.
Arguments:
- tokens: bfloat16 [32, 512, 768], P('rows', None, 'heads'), may hold values from -24 to 24
- qkv_weight: bfloat16 [2, 768, 3, 768], replicated, may hold values from -0.21875 to 0.21875
- out_weight: bfloat16 [2, 768, 768], replicated, may hold values from -0.21875 to 0.21875
- norm_gain: bfloat16 [2, 768], replicated, may hold values from 0.099609375 to 1.8984375
Outputs:
- stream: bfloat16 [32, 512, 768], P('rows', None, 'heads')
The draws below stay inside these ranges and needn't reach their ends.
All inputs are finite; a program needn't handle non-finite values.
Results may differ from the reference program's by a relative error of at most 0.0096.
Values may be sent and summed in bfloat16 or wider, within the bound.
No kernel may reach another device: no remote copies, remote signals or barrier semaphores. Data moves between devices by JAX's collectives and lax.ppermute only.
A program may use at most 64 MiB of HBM per device.

```python
import jax
import jax.numpy as jnp
from jax import lax

D = 768
HEADS = 12
HEAD_DIM = 64
RESIDUES = 512
LAYERS = 2
BLOCKS = 2
SEQS = 32


def draw_tokens(key, part):
    entries = jnp.clip(jax.random.normal(key, (SEQS, RESIDUES, D), jnp.float32), -6.0, 6.0)
    return entries.astype(jnp.bfloat16)


def gaussian(own_key, extent, deviation, bound, held_as=jnp.bfloat16):
    drawn = deviation * jax.random.normal(own_key, extent, jnp.float32)
    return jnp.clip(drawn, min=-bound, max=bound).astype(held_as)


def setup_inputs(seed: int = 0) -> dict:
    key_list = jax.random.split(jax.random.key(seed), 5)
    return {
        "tokens": draw_tokens(jax.random.fold_in(key_list[4], 71), 0),
        "qkv_weight": gaussian(key_list[1], (LAYERS, D, 3, D), D ** -0.5, 0.21875),
        "out_weight": gaussian(key_list[2], (LAYERS, D, D), D ** -0.5, 0.21875),
        "norm_gain": jnp.clip(1.0 + 0.18 * jax.random.normal(key_list[3], (LAYERS, D), jnp.float32), 0.099609375, 1.8984375).astype(jnp.bfloat16),
    }


epsilon = 1e-06

def reference(tokens, qkv_weight, out_weight, norm_gain):
    stream = tokens
    score_scale = 1.0 / (HEAD_DIM * SEQS) ** 0.5
    block_rows = RESIDUES // BLOCKS
    for layer_index in range(LAYERS):
        flattened = stream.reshape(SEQS * RESIDUES, D)
        matrix = qkv_weight[layer_index].reshape(D, 3 * D)
        projected = jnp.dot(flattened, matrix, preferred_element_type=jnp.float32).astype(jnp.bfloat16)
        projected = projected.reshape(SEQS, RESIDUES, 3, HEADS, HEAD_DIM)
        key_vecs = projected[:, :, 1].astype(jnp.float32)
        values = projected[:, :, 2].astype(jnp.float32)
        pieces_out = []
        for block_index in range(BLOCKS):
            queries = projected[:, block_index * block_rows:(block_index + 1) * block_rows, 0].astype(jnp.float32)
            scores = jnp.einsum('sihc,sjhc->hij', queries, key_vecs) * score_scale
            weights = jax.nn.softmax(scores, axis=-1).astype(jnp.bfloat16)
            attended = jnp.einsum('hij,sjhc->sihc', weights.astype(jnp.float32), values)
            pieces_out.append(attended.astype(jnp.bfloat16))
        attended = jnp.concatenate(pieces_out, axis=1).reshape(SEQS * RESIDUES, D)
        update = jnp.dot(attended, out_weight[layer_index], preferred_element_type=jnp.float32)
        summed = flattened.astype(jnp.float32) + update
        mean_sq = lax.optimization_barrier(jnp.mean(summed * summed, axis=-1, keepdims=True))
        normed = summed * lax.rsqrt(mean_sq + epsilon) * norm_gain[layer_index].astype(jnp.float32)
        stream = normed.astype(jnp.bfloat16).reshape(SEQS, RESIDUES, D)
    return stream
```

```python
import functools

import jax
import jax.numpy as jnp
from jax import lax
from jax.experimental import pallas as pl
from jax.experimental.pallas import tpu as pltpu
from jax.sharding import PartitionSpec as P

HEAD_DIM = 64
epsilon = 1e-06
VMEM_LIMIT = 40 * 1024 * 1024
F32 = jnp.float32
BF16 = jnp.bfloat16


def dot(a, b):
    return jnp.dot(a, b, preferred_element_type=F32)


def dot_t(a, b):
    return lax.dot_general(a, b, (((1,), (1,)), ((), ())), preferred_element_type=F32)


def params():
    return pltpu.CompilerParams(vmem_limit_bytes=VMEM_LIMIT)


def cost(flops, nbytes, trans=0):
    return pl.CostEstimate(flops=int(flops), bytes_accessed=int(nbytes), transcendentals=int(trans))


def nbytes(*arrays):
    return sum(a.size * a.dtype.itemsize for a in arrays)


def hold_type(rows):
    return BF16 if rows % 16 == 0 else F32


SMEM = pl.BlockSpec(memory_space=pltpu.SMEM)


def whole(array):
    return pl.BlockSpec(array.shape, lambda p, r=len(array.shape): (0,) * r)


def store_projections(pair, weight, heads, outs):
    made = [dot(rows, weight).astype(BF16) for rows in pair]
    width = heads * HEAD_DIM
    for which, out in enumerate(outs):
        for head in range(heads):
            at = which * width + head * HEAD_DIM
            out[head] = jnp.concatenate([m[:, at : at + HEAD_DIM] for m in made], axis=1)


def first_kernel(heads, place, near, far, weight, x_out, q_out, k_out, v_out):
    x_bit, core = place[0], place[1]
    quarter = near.shape[2] // 2
    pair = []
    for s in range(near.shape[0]):
        halves = []
        for ref in (near, far):
            rows = ref[s]
            swapped = jnp.concatenate([rows[:, quarter:], rows[:, :quarter]], axis=1)
            halves.append(jnp.where(core == 1, swapped, rows))
        low = jnp.where(x_bit == 1, halves[1], halves[0])
        high = jnp.where(x_bit == 1, halves[0], halves[1])
        rows = jnp.concatenate([low, high], axis=1)
        x_out[s] = rows
        pair.append(rows)
    store_projections(pair, weight[...], heads, (q_out, k_out, v_out))


def first(place, near, far, weight, heads):
    seqs, residues, half = near.shape
    width = 2 * half
    lanes = 2 * HEAD_DIM
    wide = jax.ShapeDtypeStruct((heads, residues, seqs * HEAD_DIM), BF16)
    flops = 2 * seqs * residues * width * weight.shape[1]
    piece = pl.BlockSpec((2, residues, half), lambda p: (p, 0, 0))
    out_block = pl.BlockSpec((heads, residues, lanes), lambda p: (0, 0, p))
    return pl.pallas_call(
        functools.partial(first_kernel, heads),
        grid=(seqs // 2,),
        in_specs=[SMEM, piece, piece, whole(weight)],
        out_specs=[pl.BlockSpec((2, residues, width), lambda p: (p, 0, 0))] + [out_block] * 3,
        out_shape=[jax.ShapeDtypeStruct((seqs, residues, width), BF16)] + [wide] * 3,
        compiler_params=params(),
        cost_estimate=cost(flops, 4 * nbytes(near, far) + nbytes(weight)),
    )(place, near, far, weight)


def score_kernel(scale, z_ref, *refs):
    queries, keys, others, outs, hold = refs[0:2], refs[2:4], refs[4:6], refs[6:-1], refs[-1]
    z = z_ref[0]
    heads, rows = outs[0].shape[0], outs[0].shape[1]
    residues = queries[0].shape[1]
    for head in range(heads):
        near = dot_t(queries[0][head], keys[0][head]) + dot_t(queries[1][head], keys[1][head])
        hold[:, :residues] = (near * scale).astype(hold.dtype)
        far = dot_t(queries[0][head], others[0][head]) + dot_t(queries[1][head], others[1][head])
        hold[:, residues:] = (far * scale).astype(hold.dtype)
        for d, out in enumerate(outs):
            start = pl.multiple_of(jnp.bitwise_xor(z, d) * rows, rows)
            out[head] = hold[pl.ds(start, rows), :].astype(BF16)


def score_chunks(z, queries, keys, others, scale, chunks):
    heads, residues, depth = queries[0].shape
    rows = residues // chunks
    args = (*queries, *keys, *others)
    return pl.pallas_call(
        functools.partial(score_kernel, scale),
        in_specs=[SMEM] + [pl.BlockSpec(memory_space=pltpu.VMEM)] * 6,
        out_specs=[pl.BlockSpec(memory_space=pltpu.VMEM)] * chunks,
        out_shape=[jax.ShapeDtypeStruct((heads, rows, 2 * residues), BF16)] * chunks,
        scratch_shapes=[pltpu.VMEM((residues, 2 * residues), hold_type(rows))],
        compiler_params=params(),
        cost_estimate=cost(8 * heads * residues * residues * depth, 2 * nbytes(*args)),
    )(z, *args)


def softmax_kernel(*refs):
    terms, out = refs[:-1], refs[-1]
    total = terms[0][...].astype(F32)
    for term in terms[1:]:
        total = total + term[...].astype(F32)
    top = jnp.max(total, axis=-1, keepdims=True)
    grown = jnp.exp(total - top)
    out[...] = (grown / jnp.sum(grown, axis=-1, keepdims=True)).astype(BF16)


def softmax_sum(terms):
    return pl.pallas_call(
        softmax_kernel,
        out_shape=jax.ShapeDtypeStruct(terms[0].shape, BF16),
        compiler_params=params(),
        cost_estimate=cost(10 * terms[0].size, nbytes(*terms), terms[0].size),
    )(*terms)


def value_kernel(chunks, z_ref, *refs):
    pieces, values, others = refs[:chunks], refs[chunks : chunks + 2], refs[chunks + 2 : chunks + 4]
    outs, hold = refs[chunks + 4 : chunks + 6], refs[-1]
    z = z_ref[0]
    heads, rows = pieces[0].shape[0], pieces[0].shape[1]
    residues = values[0].shape[1]
    for head in range(heads):
        for d, piece in enumerate(pieces):
            start = pl.multiple_of(jnp.bitwise_xor(z, d) * rows, rows)
            hold[pl.ds(start, rows), :] = piece[head].astype(hold.dtype)
        near, far = hold[:, :residues].astype(BF16), hold[:, residues:].astype(BF16)
        for value, other, out in zip(values, others, outs):
            out[head] = (dot(near, value[head]) + dot(far, other[head])).astype(BF16)


def weighted_values(z, pieces, values, others):
    heads, residues, depth = values[0].shape
    args = (*pieces, *values, *others)
    return pl.pallas_call(
        functools.partial(value_kernel, len(pieces)),
        in_specs=[SMEM] + [pl.BlockSpec(memory_space=pltpu.VMEM)] * len(args),
        out_specs=[pl.BlockSpec(memory_space=pltpu.VMEM)] * 2,
        out_shape=[jax.ShapeDtypeStruct((heads, residues, depth), BF16)] * 2,
        scratch_shapes=[pltpu.VMEM((residues, 2 * residues), hold_type(pieces[0].shape[1]))],
        compiler_params=params(),
        cost_estimate=cost(8 * heads * residues * residues * depth, 2 * nbytes(*args)),
    )(z, *args)


def normalized(attended, x, out_weight, gain, s):
    columns = [
        ref[head][:, s * HEAD_DIM : (s + 1) * HEAD_DIM] for ref in attended for head in range(ref.shape[0])
    ]
    rows = jnp.concatenate(columns, axis=1)
    summed = x[s].astype(F32) + dot(rows, out_weight[...])
    mean_sq = jnp.mean(summed * summed, axis=-1, keepdims=True)
    return summed * lax.rsqrt(mean_sq + epsilon) * gain[...].astype(F32)


def next_kernel(heads, a0, a1, a2, a3, x, out_weight, gain, weight, x_out, q_out, k_out, v_out):
    pair = []
    for s in range(2):
        rows = normalized((a0, a1, a2, a3), x, out_weight, gain, s).astype(BF16)
        x_out[s] = rows
        pair.append(rows)
    store_projections(pair, weight[...], heads, (q_out, k_out, v_out))


def next_layer(attended, x, out_weight, gain, weight):
    seqs, residues, width = x.shape
    heads = attended[0].shape[0]
    lanes = 2 * HEAD_DIM
    wide = jax.ShapeDtypeStruct((heads, residues, seqs * HEAD_DIM), BF16)
    block = pl.BlockSpec((heads, residues, lanes), lambda p: (0, 0, p))
    x_block = pl.BlockSpec((2, residues, width), lambda p: (p, 0, 0))
    flops = 2 * seqs * residues * width * (weight.shape[1] + width)
    return pl.pallas_call(
        functools.partial(next_kernel, heads),
        grid=(seqs // 2,),
        in_specs=[block] * 4 + [x_block, whole(out_weight), whole(gain), whole(weight)],
        out_specs=[x_block] + [block] * 3,
        out_shape=[jax.ShapeDtypeStruct(x.shape, BF16)] + [wide] * 3,
        compiler_params=params(),
        cost_estimate=cost(flops, 4 * nbytes(x) + nbytes(out_weight, weight)),
    )(*attended, x, out_weight, gain, weight)


def last_kernel(place, a0, a1, a2, a3, x, out_weight, gain, keep, send):
    x_bit, core = place[0], place[1]
    quarter = keep.shape[2]
    for s in range(2):
        rows = normalized((a0, a1, a2, a3), x, out_weight, gain, s)
        half = jnp.where(x_bit == 1, rows[:, 2 * quarter :], rows[:, : 2 * quarter])
        low, high = half[:, :quarter], half[:, quarter:]
        keep[s] = jnp.where(core == 1, high, low).astype(BF16)
        send[s] = jnp.where(core == 1, low, high).astype(BF16)


def last_layer(place, attended, x, out_weight, gain):
    seqs, residues, width = x.shape
    heads = attended[0].shape[0]
    block = pl.BlockSpec((heads, residues, 2 * HEAD_DIM), lambda p: (0, 0, p))
    x_block = pl.BlockSpec((2, residues, width), lambda p: (p, 0, 0))
    out_block = pl.BlockSpec((2, residues, width // 4), lambda p: (p, 0, 0))
    return pl.pallas_call(
        last_kernel,
        grid=(seqs // 2,),
        in_specs=[SMEM] + [block] * 4 + [x_block, whole(out_weight), whole(gain)],
        out_specs=[out_block] * 2,
        out_shape=[jax.ShapeDtypeStruct((seqs, residues, width // 4), BF16)] * 2,
        compiler_params=params(),
        cost_estimate=cost(2 * seqs * residues * width * width, 3 * nbytes(x) + nbytes(out_weight)),
    )(place, *attended, x, out_weight, gain)


def on_device(tokens, qkv_weight, out_weight, norm_gain):
    seqs, residues, _ = tokens.shape
    layers, width = norm_gain.shape
    n_rows, n_groups = lax.axis_size("rows"), lax.axis_size("heads")
    all_heads = width // HEAD_DIM
    row, group = lax.axis_index("rows"), lax.axis_index("heads")
    core, x_bit = group % 2, group // 2
    y_bit, z = row % 2, row // 2
    depth = n_rows // 2
    own = x_bit * 2 + y_bit
    heads = all_heads // 4
    own_width = heads * HEAD_DIM
    half = residues // 2
    scale = 1.0 / (HEAD_DIM * seqs * n_rows) ** 0.5
    place = jnp.stack([x_bit, core]).astype(jnp.int32)
    z_at = z.astype(jnp.int32).reshape(1)

    def over_core(a):
        return lax.ppermute(a, "heads", [(i, i ^ 1) for i in range(n_groups)])

    def over_x(a):
        return lax.ppermute(a, "heads", [(i, i ^ 2) for i in range(n_groups)])

    def over_y(a):
        return lax.ppermute(a, "rows", [(i, i ^ 1) for i in range(n_rows)])

    def over_z(a, d):
        return lax.ppermute(a, "rows", [(i, i ^ (2 * d)) for i in range(n_rows)])

    def own_columns(layer):
        columns = lax.dynamic_slice_in_dim(qkv_weight[layer], own * own_width, own_width, 2)
        return columns.reshape(width, 3 * own_width)

    def out_rows(layer):
        parts = [
            lax.dynamic_slice_in_dim(out_weight[layer], (own ^ d) * own_width, own_width, 0)
            for d in (0, 2, 1, 3)
        ]
        return jnp.concatenate(parts, axis=0)

    mine = lax.dynamic_slice_in_dim(tokens, core * half, half, 1)
    theirs = lax.dynamic_slice_in_dim(tokens, (1 - core) * half, half, 1)
    packed = jnp.concatenate([mine, over_core(theirs)], axis=2)
    cut = seqs // 2
    lows, highs = packed[:cut], packed[cut:]
    x_low, x_high = over_x(lows), over_x(highs)
    y_low, y_high = over_y(lows), over_y(highs)
    d_low, d_high = over_y(x_low), over_x(y_high)
    weight = own_columns(0)
    streams, queries, keys, values = [], [], [], []
    for near, far in (
        (packed, jnp.concatenate([x_low, x_high])),
        (jnp.concatenate([y_low, y_high]), jnp.concatenate([d_low, d_high])),
    ):
        made = first(place, near, far, weight, heads)
        for kept, one in zip((streams, queries, keys, values), made):
            kept.append(one)

    for layer in range(layers):
        other_keys = [over_core(k) for k in keys]
        other_values = [over_core(v) for v in values]
        chunks = score_chunks(z_at, queries, keys, other_keys, scale, depth)
        terms = [chunks[0]] + [over_z(chunks[d], d) for d in range(1, depth)]
        weights = softmax_sum(terms)
        pieces = [weights] + [over_z(weights, d) for d in range(1, depth)]
        near, far = weighted_values(z_at, pieces, values, other_values)
        gain = norm_gain[layer : layer + 1]
        if layer + 1 < layers:
            x_near, x_far = over_x(near), over_x(far)
            y_far, y_near = over_y(near), over_y(far)
            d_far = over_y(x_near)
            d_near = over_x(y_near)
            weight, out_mat = own_columns(layer + 1), out_rows(layer)
            queries, keys, values, new_streams = [], [], [], []
            for attended, x in (
                ((near, x_near, y_near, d_near), streams[0]),
                ((far, x_far, y_far, d_far), streams[1]),
            ):
                made = next_layer(attended, x, out_mat, gain, weight)
                for kept, one in zip((new_streams, queries, keys, values), made):
                    kept.append(one)
            streams = new_streams
        else:
            x_near, y_near = over_x(near), over_y(far)
            d_near = over_x(y_near)
            keep, send = last_layer(
                place, (near, x_near, y_near, d_near), streams[0], out_rows(layer), gain
            )
    other = over_core(send)
    ordered = [jnp.where(core == 0, keep, other), jnp.where(core == 0, other, keep)]
    return jnp.concatenate(ordered, axis=1)


def solution(mesh):
    return jax.shard_map(
        on_device,
        mesh=mesh,
        in_specs=(P("rows", None, "heads"), P(), P(), P()),
        out_specs=P("rows", None, "heads"),
        check_vma=False,
    )
```

```python
import functools

import jax
import jax.numpy as jnp
from jax import lax
from jax.experimental import pallas as pl
from jax.experimental.pallas import tpu as pltpu
from jax.sharding import PartitionSpec as P

HEAD_DIM = 64
epsilon = 1e-06
VMEM_LIMIT = 12 * 1024 * 1024
PIECES = 2
F32 = jnp.float32
BF16 = jnp.bfloat16


def dot(a, b):
    return jnp.dot(a, b, preferred_element_type=F32)


def dot_t(a, b):
    return lax.dot_general(a, b, (((1,), (1,)), ((), ())), preferred_element_type=F32)


def params():
    return pltpu.CompilerParams(vmem_limit_bytes=VMEM_LIMIT)


def cost(flops, nbytes, trans=0):
    return pl.CostEstimate(flops=int(flops), bytes_accessed=int(nbytes), transcendentals=int(trans))


def nbytes(*arrays):
    return sum(a.size * a.dtype.itemsize for a in arrays)


def hold_type(rows):
    return BF16 if rows % 16 == 0 else F32


SMEM = pl.BlockSpec(memory_space=pltpu.SMEM)


FULL = pl.BlockSpec(memory_space=pltpu.VMEM)


def store_projections(rows, weights, parts, lane, outs):
    count = rows.shape[0] // parts
    for weight, out in zip(weights, outs):
        projected = dot(rows, weight[...]).astype(BF16)
        for head in range(out.shape[0]):
            at = head * HEAD_DIM
            out[head, :, lane : lane + parts * HEAD_DIM] = jnp.concatenate(
                [projected[n * count : (n + 1) * count, at : at + HEAD_DIM] for n in range(parts)], axis=1
            )


def first_kernel(place, p0, p1, p2, p3, *refs):
    weights, x_out, outs = refs[:3], refs[3], refs[4:]
    x_bit, core = place[0], place[1]
    quarter = p0.shape[2] // 2
    for p in range(p0.shape[0]):
        pair = []
        for s in range(2):
            parts = [ref[p][:, s * quarter : (s + 1) * quarter] for ref in (p0, p1, p2, p3)]
            swapped = [jnp.where(core == 1, parts[t ^ 1], parts[t]) for t in range(4)]
            rows = jnp.concatenate(
                [jnp.where(x_bit == 1, swapped[t ^ 2], swapped[t]) for t in range(4)], axis=1
            )
            x_out[2 * p + s] = rows
            pair.append(rows)
        store_projections(jnp.concatenate(pair, axis=0), weights, 2, 2 * p * HEAD_DIM, outs)


def first(place, pieces, weights, heads):
    pairs, residues, half = pieces[0].shape
    width = 2 * half
    wide = jax.ShapeDtypeStruct((heads, residues, 2 * pairs * HEAD_DIM), BF16)
    flops = 12 * pairs * residues * width * weights[0].shape[1]
    return pl.pallas_call(
        first_kernel,
        in_specs=[SMEM] + [FULL] * 7,
        out_specs=[FULL] * 4,
        out_shape=[jax.ShapeDtypeStruct((2 * pairs, residues, width), BF16)] + [wide] * 3,
        compiler_params=params(),
        cost_estimate=cost(flops, 4 * nbytes(*pieces, *weights)),
    )(place, *pieces, *weights)


def score_kernel(scale, place, *refs):
    queries, keys, others, outs, hold = refs[0:2], refs[2:4], refs[4:6], refs[6:-1], refs[-1]
    z = place[2]
    heads, rows = outs[0].shape[0], outs[0].shape[1]
    residues = queries[0].shape[1]
    for head in range(heads):
        near = dot_t(queries[0][head], keys[0][head]) + dot_t(queries[1][head], keys[1][head])
        hold[:, :residues] = (near * scale).astype(hold.dtype)
        far = dot_t(queries[0][head], others[0][head]) + dot_t(queries[1][head], others[1][head])
        hold[:, residues:] = (far * scale).astype(hold.dtype)
        for d, out in enumerate(outs):
            start = pl.multiple_of(jnp.bitwise_xor(z, d) * rows, rows)
            out[head] = hold[pl.ds(start, rows), :].astype(BF16)


def score_chunks(place, queries, keys, others, scale, chunks):
    heads, residues, depth = queries[0].shape
    rows = residues // chunks
    args = (*queries, *keys, *others)
    return pl.pallas_call(
        functools.partial(score_kernel, scale),
        in_specs=[SMEM] + [FULL] * 6,
        out_specs=[FULL] * chunks,
        out_shape=[jax.ShapeDtypeStruct((heads, rows, 2 * residues), BF16)] * chunks,
        scratch_shapes=[pltpu.VMEM((residues, 2 * residues), hold_type(rows))],
        compiler_params=params(),
        cost_estimate=cost(8 * heads * residues * residues * depth, 2 * nbytes(*args)),
    )(place, *args)


def joined_score_kernel(scale, count, place, *refs):
    queries, keys, others = (refs[i * count : (i + 1) * count] for i in range(3))
    outs, key_hold, hold = refs[3 * count : -2], refs[-2], refs[-1]
    high, low = place[3], place[4]
    heads, rows = outs[0].shape[0], outs[0].shape[1]
    piece_rows = queries[0].shape[1]
    each = piece_rows // rows
    residues = count * piece_rows
    for head in range(heads):
        for side, group in enumerate((keys, others)):
            for g, ref in enumerate(group):
                start = side * residues + jnp.bitwise_xor(high, g) * piece_rows
                key_hold[pl.ds(pl.multiple_of(start, piece_rows), piece_rows), :] = ref[head]
        query = jnp.concatenate([ref[head] for ref in queries], axis=0)
        scores = dot_t(query, key_hold[...]) * scale
        if each == 1:
            for g, out in enumerate(outs):
                out[head] = scores[g * rows : (g + 1) * rows].astype(BF16)
        else:
            hold[...] = scores.astype(hold.dtype)
            for d, out in enumerate(outs):
                start = (d // each) * piece_rows + jnp.bitwise_xor(low, d % each) * rows
                out[head] = hold[pl.ds(pl.multiple_of(start, rows), rows), :].astype(BF16)


def joined_score_chunks(place, queries, keys, others, scale, chunks):
    heads, piece_rows, depth = queries[0].shape
    count = len(queries)
    residues = count * piece_rows
    rows = residues // chunks
    args = (*queries, *keys, *others)
    return pl.pallas_call(
        functools.partial(joined_score_kernel, scale, count),
        in_specs=[SMEM] + [FULL] * len(args),
        out_specs=[FULL] * chunks,
        out_shape=[jax.ShapeDtypeStruct((heads, rows, 2 * residues), BF16)] * chunks,
        scratch_shapes=[
            pltpu.VMEM((2 * residues, depth), BF16),
            pltpu.VMEM((residues, 2 * residues), hold_type(rows)),
        ],
        compiler_params=params(),
        cost_estimate=cost(4 * heads * residues * residues * depth, 2 * nbytes(*args)),
    )(place, *args)


def softmax_kernel(*refs):
    terms, out = refs[:-1], refs[-1]
    total = terms[0][...].astype(F32)
    for term in terms[1:]:
        total = total + term[...].astype(F32)
    top = jnp.max(total, axis=-1, keepdims=True)
    grown = jnp.exp(total - top)
    out[...] = (grown / jnp.sum(grown, axis=-1, keepdims=True)).astype(BF16)


def softmax_sum(terms):
    return pl.pallas_call(
        softmax_kernel,
        out_shape=jax.ShapeDtypeStruct(terms[0].shape, BF16),
        compiler_params=params(),
        cost_estimate=cost(10 * terms[0].size, nbytes(*terms), terms[0].size),
    )(*terms)


def lane_blocks(pairs):
    return [(pair, side) for pair in range(pairs) for side in range(2)]


def gather_first_kernel(near, far, other_near, other_far, out):
    residues = near.shape[1]
    lanes = 2 * HEAD_DIM
    for n, (pair, side) in enumerate(lane_blocks(near.shape[2] // lanes)):
        at = slice(pair * lanes, (pair + 1) * lanes)
        out[:, :residues, n * lanes : (n + 1) * lanes] = (near, far)[side][:, :, at]
        out[:, residues:, n * lanes : (n + 1) * lanes] = (other_near, other_far)[side][:, :, at]


def gather_first(values, others):
    heads, residues, depth = values[0].shape
    return pl.pallas_call(
        gather_first_kernel,
        out_shape=jax.ShapeDtypeStruct((heads, 2 * residues, 2 * depth), BF16),
        compiler_params=params(),
        cost_estimate=cost(0, 4 * nbytes(*values)),
    )(*values, *others)


def gather_kernel(count, place, *refs):
    out = refs[-1]
    rows = refs[0].shape[1]
    for n, ref in enumerate(refs[:-1]):
        start = (n // count) * count * rows + jnp.bitwise_xor(place[3], n % count) * rows
        out[:, pl.ds(pl.multiple_of(start, rows), rows), :] = ref[...]


def gather(place, values, others):
    heads, rows, depth = values[0].shape
    count = len(values)
    return pl.pallas_call(
        functools.partial(gather_kernel, count),
        in_specs=[SMEM] + [FULL] * (2 * count),
        out_specs=FULL,
        out_shape=jax.ShapeDtypeStruct((heads, 2 * count * rows, depth), BF16),
        compiler_params=params(),
        cost_estimate=cost(0, 4 * nbytes(*values)),
    )(place, *values, *others)


def value_kernel(count, place, *refs):
    pieces, values, outs, hold = refs[:count], refs[count], refs[count + 1 : -1], refs[-1]
    heads, rows = pieces[0].shape[0], pieces[0].shape[1]
    lanes = 2 * HEAD_DIM
    for head in range(heads):
        if count == 1:
            weights = pieces[0][head]
        else:
            for e, piece in enumerate(pieces):
                start = pl.multiple_of(jnp.bitwise_xor(place[4], e) * rows, rows)
                hold[pl.ds(start, rows), :] = piece[head].astype(hold.dtype)
            weights = hold[...].astype(BF16)
        made = dot(weights, values[head]).astype(BF16)
        for n, (pair, side) in enumerate(lane_blocks(made.shape[1] // (2 * lanes))):
            outs[side][head, :, pair * lanes : (pair + 1) * lanes] = made[:, n * lanes : (n + 1) * lanes]


def weighted_values(place, pieces, values):
    heads, rows, residues = pieces[0].shape
    depth = values.shape[2]
    rows *= len(pieces)
    return pl.pallas_call(
        functools.partial(value_kernel, len(pieces)),
        in_specs=[SMEM] + [FULL] * (len(pieces) + 1),
        out_specs=[FULL] * 2,
        out_shape=[jax.ShapeDtypeStruct((heads, rows, depth // 2), BF16)] * 2,
        scratch_shapes=[pltpu.VMEM((rows, residues), hold_type(pieces[0].shape[1]))],
        compiler_params=params(),
        cost_estimate=cost(2 * heads * rows * residues * depth, nbytes(*pieces, values)),
    )(place, *pieces, values)


def normalized(rows, x, out_weight, gain):
    summed = x.astype(F32) + dot(rows, out_weight[...])
    mean_sq = jnp.mean(summed * summed, axis=-1, keepdims=True)
    return summed * lax.rsqrt(mean_sq + epsilon) * gain[...].astype(F32)


def head_columns(refs, lane):
    return jnp.concatenate(
        [ref[head][:, lane : lane + HEAD_DIM] for ref in refs for head in range(ref.shape[0])],
        axis=1,
    )


def next_kernel(g, place, *refs):
    attended_refs, (near, far, out_weight, gain), weights, outs = refs[:8], refs[8:12], refs[12:15], refs[15:]
    streams, projections = outs[:-3], outs[-3:]
    rows, depth = attended_refs[0].shape[1:]
    parts = [(side, s) for side in range(2) for s in range(2)]
    start = 0
    if near.shape[1] != rows:
        start = pl.multiple_of(jnp.bitwise_xor(place[3], g) * rows, rows)
    for p in range(depth // (2 * HEAD_DIM)):
        attended = [
            head_columns(attended_refs[4 * side : 4 * side + 4], (2 * p + s) * HEAD_DIM) for side, s in parts
        ]
        x = jnp.concatenate(
            [(near, far)[side][2 * p + s, pl.ds(start, rows), :] for side, s in parts], axis=0
        )
        made = normalized(jnp.concatenate(attended, axis=0), x, out_weight, gain).astype(BF16)
        for n, (side, s) in enumerate(parts):
            if side < len(streams):
                streams[side][2 * p + s] = made[n * rows : (n + 1) * rows]
        store_projections(made, weights, len(parts), p * len(parts) * HEAD_DIM, projections)


def next_layer(place, g, attended, near, far, out_weight, gain, weights, both):
    seqs, _, width = near.shape
    heads, rows, depth = attended[0].shape
    depth *= 2
    streams = 2 if both else 1
    flops = 4 * seqs * rows * width * (3 * weights[0].shape[1] + width)
    return pl.pallas_call(
        functools.partial(next_kernel, g),
        in_specs=[SMEM] + [FULL] * 15,
        out_specs=[FULL] * (streams + 3),
        out_shape=[jax.ShapeDtypeStruct((seqs, rows, width), BF16)] * streams
        + [jax.ShapeDtypeStruct((heads, rows, depth), BF16)] * 3,
        compiler_params=params(),
        cost_estimate=cost(flops, 8 * seqs * rows * width + nbytes(out_weight, *weights)),
    )(place, *attended, near, far, out_weight, gain, *weights)


def last_kernel(place, a0, a1, a2, a3, x, out_weight, gain, keep, send):
    x_bit, core = place[0], place[1]
    seqs, rows, _ = x.shape
    quarter = keep.shape[3]
    columns = [head_columns((a0, a1, a2, a3), s * HEAD_DIM) for s in range(seqs)]
    old = jnp.concatenate([x[s] for s in range(seqs)], axis=0)
    made = normalized(jnp.concatenate(columns, axis=0), old, out_weight, gain)
    half = jnp.where(x_bit == 1, made[:, 2 * quarter :], made[:, : 2 * quarter]).astype(BF16)
    low, high = half[:, :quarter], half[:, quarter:]
    mine, theirs = jnp.where(core == 1, high, low), jnp.where(core == 1, low, high)
    for s in range(seqs):
        keep[s % 2, s // 2] = mine[s * rows : (s + 1) * rows]
        send[s % 2, s // 2] = theirs[s * rows : (s + 1) * rows]


def last_layer(place, attended, x, out_weight, gain):
    seqs, rows, width = x.shape
    made = pl.pallas_call(
        last_kernel,
        in_specs=[SMEM] + [FULL] * 7,
        out_specs=[FULL] * 2,
        out_shape=[jax.ShapeDtypeStruct((2, seqs // 2, rows, width // 4), BF16)] * 2,
        compiler_params=params(),
        cost_estimate=cost(2 * seqs * rows * width * width, 3 * nbytes(x) + nbytes(out_weight)),
    )(place, *attended, x, out_weight, gain)
    return [a.reshape(seqs, rows, width // 4) for a in made]


def placed_kernel(count, place, *refs):
    out = refs[-1]
    rows = refs[0].shape[1]
    for n, ref in enumerate(refs[:-1]):
        core = jnp.bitwise_xor(place[1], n // count)
        start = (core * count + jnp.bitwise_xor(place[3], n % count)) * rows
        out[:, pl.ds(pl.multiple_of(start, rows), rows), :] = ref[...]


def placed(place, kept, other):
    seqs, rows, width = kept[0].shape
    count = len(kept)
    piece = pl.BlockSpec((2, rows, width), lambda s: (s, 0, 0))
    return pl.pallas_call(
        functools.partial(placed_kernel, count),
        grid=(seqs // 2,),
        in_specs=[SMEM] + [piece] * (2 * count),
        out_specs=pl.BlockSpec((2, 2 * count * rows, width), lambda s: (s, 0, 0)),
        out_shape=jax.ShapeDtypeStruct((seqs, 2 * count * rows, width), BF16),
        compiler_params=params(),
        cost_estimate=cost(0, 4 * nbytes(*kept)),
    )(place, *kept, *other)


def on_device(tokens, qkv_weight, out_weight, norm_gain):
    seqs, residues, _ = tokens.shape
    layers, width = norm_gain.shape
    n_rows, n_groups = lax.axis_size("rows"), lax.axis_size("heads")
    all_heads = width // HEAD_DIM
    row, group = lax.axis_index("rows"), lax.axis_index("heads")
    core, x_bit = group % 2, group // 2
    y_bit, z = row % 2, row // 2
    depth = n_rows // 2
    own = x_bit * 2 + y_bit
    heads = all_heads // 4
    own_width = heads * HEAD_DIM
    half = residues // 2
    scale = 1.0 / (HEAD_DIM * seqs * n_rows) ** 0.5
    count = min(depth, PIECES)
    each = depth // count
    place = jnp.stack([x_bit, core, z, z // each, z % each]).astype(jnp.int32)

    def over_core(a):
        return lax.ppermute(a, "heads", [(i, i ^ 1) for i in range(n_groups)])

    def over_x(a):
        return lax.ppermute(a, "heads", [(i, i ^ 2) for i in range(n_groups)])

    def over_y(a):
        return lax.ppermute(a, "rows", [(i, i ^ 1) for i in range(n_rows)])

    def over_z(a, d):
        return lax.ppermute(a, "rows", [(i, i ^ (2 * d)) for i in range(n_rows)])

    def own_columns(layer, at):
        return tuple(
            lax.dynamic_slice(
                qkv_weight, (layer, 0, which, at * own_width), (1, width, 1, own_width)
            ).reshape(width, own_width)
            for which in range(qkv_weight.shape[2])
        )

    def out_rows(layer, at):
        parts = [
            lax.dynamic_slice(out_weight, (layer, (at ^ d) * own_width, 0), (1, own_width, width))[0]
            for d in (0, 2, 1, 3)
        ]
        return jnp.concatenate(parts, axis=0)

    def packed(which):
        part = lax.dynamic_slice_in_dim(tokens, which * half, half, 1)
        return jnp.concatenate([part[: seqs // 2], part[seqs // 2 :]], axis=2)

    mine = packed(core)
    sibling = over_core(packed(1 - core))
    x_mine, y_mine = over_x(mine), over_y(mine)
    x_sibling, y_sibling = over_x(sibling), over_y(sibling)
    d_mine, d_sibling = over_y(x_mine), over_x(y_sibling)
    weight = own_columns(0, own)
    streams, queries, keys, values = [], [], [], []
    for pieces in ((mine, sibling, x_mine, x_sibling), (y_mine, y_sibling, d_mine, d_sibling)):
        made = first(place, pieces, weight, heads)
        for kept, one in zip((streams, queries, keys, values), made):
            kept.append(one)
    near, far = [streams[0]] * count, [streams[1]] * count

    for layer in range(layers):
        more = layer + 1 < layers
        other_keys = [over_core(k) for k in keys]
        other_values = [over_core(v) for v in values]
        if layer == 0:
            chunks = score_chunks(place, queries, keys, other_keys, scale, depth)
        else:
            chunks = joined_score_chunks(place, queries, keys, other_keys, scale, depth)
        terms = [chunks[0]] + [over_z(chunks[d], d) for d in range(1, depth)]
        if layer == 0:
            value = gather_first(values, other_values)
        else:
            value = gather(place, values, other_values)
        own_late, kept = lax.optimization_barrier((own, chunks[0]))
        out_mat = out_rows(layer, own_late)
        weight = own_columns(layer + 1, own_late) if more else ()
        terms[0], out_mat, weight, value = lax.optimization_barrier((kept, out_mat, weight, value))
        weights = softmax_sum(terms)
        gain = norm_gain[layer : layer + 1]
        pieces = [weights] + [over_z(weights, d) for d in range(1, depth)]
        attended = []
        for g in range(count):
            near_part, far_part = weighted_values(place, pieces[g * each : (g + 1) * each], value)
            if g:
                before = attended[-1]
                near_part, far_part, before[1], before[2] = lax.optimization_barrier(
                    (near_part, far_part, before[1], before[2])
                )
            x_near, y_near = over_x(near_part), over_y(far_part)
            parts = [near_part, x_near, y_near, over_x(y_near)]
            if more:
                parts += [far_part, over_x(far_part), over_y(near_part), over_y(x_near)]
            attended.append(parts)
        if more:
            both = layer + 2 < layers
            made = [
                next_layer(place, g, attended[g], near[g], far[g], out_mat, gain, weight, both)
                for g in range(count)
            ]
            near = [m[0] for m in made]
            far = [m[1] for m in made] if both else near
            queries, keys, values = ([m[i] for m in made] for i in (-3, -2, -1))
    kept, other = [], []
    for g in range(count):
        keep, send = last_layer(place, attended[g], near[g], out_mat, gain)
        kept.append(keep)
        other.append(over_core(send))
    return placed(place, kept, other)


def solution(mesh):
    return jax.shard_map(
        on_device,
        mesh=mesh,
        in_specs=(P("rows", None, "heads"), P(), P(), P()),
        out_specs=P("rows", None, "heads"),
        check_vma=False,
    )
```

```python
import functools

import jax
import jax.numpy as jnp
from jax import lax
from jax.experimental import pallas as pl
from jax.experimental.pallas import tpu as pltpu
from jax.sharding import PartitionSpec as P

HEAD_DIM = 64
epsilon = 1e-06
VMEM_LIMIT = 12 * 1024 * 1024
PIECES = 2
F32 = jnp.float32
BF16 = jnp.bfloat16


def dot(a, b):
    return jnp.dot(a, b, preferred_element_type=F32)


def dot_t(a, b):
    return lax.dot_general(a, b, (((1,), (1,)), ((), ())), preferred_element_type=F32)


def params():
    return pltpu.CompilerParams(vmem_limit_bytes=VMEM_LIMIT)


def cost(flops, nbytes, trans=0):
    return pl.CostEstimate(flops=int(flops), bytes_accessed=int(nbytes), transcendentals=int(trans))


def nbytes(*arrays):
    return sum(a.size * a.dtype.itemsize for a in arrays)


def hold_type(rows):
    return BF16 if rows % 16 == 0 else F32


SMEM = pl.BlockSpec(memory_space=pltpu.SMEM)


FULL = pl.BlockSpec(memory_space=pltpu.VMEM)


def store_projections(rows, weights, parts, lane, outs):
    count = rows.shape[0] // parts
    for weight, out in zip(weights, outs):
        projected = dot(rows, weight[...]).astype(BF16)
        for head in range(out.shape[0]):
            at = head * HEAD_DIM
            out[head, :, lane : lane + parts * HEAD_DIM] = jnp.concatenate(
                [projected[n * count : (n + 1) * count, at : at + HEAD_DIM] for n in range(parts)], axis=1
            )


def first_kernel(place, p0, p1, p2, p3, *refs):
    weights, x_out, outs = refs[:3], refs[3], refs[4:]
    x_bit, core = place[0], place[1]
    quarter = p0.shape[2] // 2
    for p in range(p0.shape[0]):
        pair = []
        for s in range(2):
            parts = [ref[p][:, s * quarter : (s + 1) * quarter] for ref in (p0, p1, p2, p3)]
            swapped = [jnp.where(core == 1, parts[t ^ 1], parts[t]) for t in range(4)]
            rows = jnp.concatenate(
                [jnp.where(x_bit == 1, swapped[t ^ 2], swapped[t]) for t in range(4)], axis=1
            )
            x_out[2 * p + s] = rows
            pair.append(rows)
        store_projections(jnp.concatenate(pair, axis=0), weights, 2, 2 * p * HEAD_DIM, outs)


def first(place, pieces, weights, heads):
    pairs, residues, half = pieces[0].shape
    width = 2 * half
    wide = jax.ShapeDtypeStruct((heads, residues, 2 * pairs * HEAD_DIM), BF16)
    flops = 12 * pairs * residues * width * weights[0].shape[1]
    return pl.pallas_call(
        first_kernel,
        in_specs=[SMEM] + [FULL] * 7,
        out_specs=[FULL] * 4,
        out_shape=[jax.ShapeDtypeStruct((2 * pairs, residues, width), BF16)] + [wide] * 3,
        compiler_params=params(),
        cost_estimate=cost(flops, 4 * nbytes(*pieces, *weights)),
    )(place, *pieces, *weights)


def score_kernel(scale, place, *refs):
    queries, keys, others, outs, hold = refs[0:2], refs[2:4], refs[4:6], refs[6:-1], refs[-1]
    z = place[2]
    heads, rows = outs[0].shape[0], outs[0].shape[1]
    residues = queries[0].shape[1]
    for head in range(heads):
        near = dot_t(queries[0][head], keys[0][head]) + dot_t(queries[1][head], keys[1][head])
        hold[:, :residues] = (near * scale).astype(hold.dtype)
        far = dot_t(queries[0][head], others[0][head]) + dot_t(queries[1][head], others[1][head])
        hold[:, residues:] = (far * scale).astype(hold.dtype)
        for d, out in enumerate(outs):
            start = pl.multiple_of(jnp.bitwise_xor(z, d) * rows, rows)
            out[head] = hold[pl.ds(start, rows), :].astype(BF16)


def score_chunks(place, queries, keys, others, scale, chunks):
    heads, residues, depth = queries[0].shape
    rows = residues // chunks
    args = (*queries, *keys, *others)
    return pl.pallas_call(
        functools.partial(score_kernel, scale),
        in_specs=[SMEM] + [FULL] * 6,
        out_specs=[FULL] * chunks,
        out_shape=[jax.ShapeDtypeStruct((heads, rows, 2 * residues), BF16)] * chunks,
        scratch_shapes=[pltpu.VMEM((residues, 2 * residues), hold_type(rows))],
        compiler_params=params(),
        cost_estimate=cost(8 * heads * residues * residues * depth, 2 * nbytes(*args)),
    )(place, *args)


def joined_score_kernel(scale, count, place, *refs):
    queries, keys, others = (refs[i * count : (i + 1) * count] for i in range(3))
    outs, key_hold, hold = refs[3 * count : -2], refs[-2], refs[-1]
    high, low = place[3], place[4]
    heads, rows = outs[0].shape[0], outs[0].shape[1]
    piece_rows = queries[0].shape[1]
    each = piece_rows // rows
    residues = count * piece_rows
    for head in range(heads):
        for side, group in enumerate((keys, others)):
            for g, ref in enumerate(group):
                start = side * residues + jnp.bitwise_xor(high, g) * piece_rows
                key_hold[pl.ds(pl.multiple_of(start, piece_rows), piece_rows), :] = ref[head]
        query = jnp.concatenate([ref[head] for ref in queries], axis=0)
        scores = dot_t(query, key_hold[...]) * scale
        if each == 1:
            for g, out in enumerate(outs):
                out[head] = scores[g * rows : (g + 1) * rows].astype(BF16)
        else:
            hold[...] = scores.astype(hold.dtype)
            for d, out in enumerate(outs):
                start = (d // each) * piece_rows + jnp.bitwise_xor(low, d % each) * rows
                out[head] = hold[pl.ds(pl.multiple_of(start, rows), rows), :].astype(BF16)


def joined_score_chunks(place, queries, keys, others, scale, chunks):
    heads, piece_rows, depth = queries[0].shape
    count = len(queries)
    residues = count * piece_rows
    rows = residues // chunks
    args = (*queries, *keys, *others)
    return pl.pallas_call(
        functools.partial(joined_score_kernel, scale, count),
        in_specs=[SMEM] + [FULL] * len(args),
        out_specs=[FULL] * chunks,
        out_shape=[jax.ShapeDtypeStruct((heads, rows, 2 * residues), BF16)] * chunks,
        scratch_shapes=[
            pltpu.VMEM((2 * residues, depth), BF16),
            pltpu.VMEM((residues, 2 * residues), hold_type(rows)),
        ],
        compiler_params=params(),
        cost_estimate=cost(4 * heads * residues * residues * depth, 2 * nbytes(*args)),
    )(place, *args)


def softmax_kernel(*refs):
    terms, out = refs[:-1], refs[-1]
    total = terms[0][...].astype(F32)
    for term in terms[1:]:
        total = total + term[...].astype(F32)
    top = jnp.max(total, axis=-1, keepdims=True)
    grown = jnp.exp(total - top)
    out[...] = (grown / jnp.sum(grown, axis=-1, keepdims=True)).astype(BF16)


def softmax_sum(terms):
    return pl.pallas_call(
        softmax_kernel,
        out_shape=jax.ShapeDtypeStruct(terms[0].shape, BF16),
        compiler_params=params(),
        cost_estimate=cost(10 * terms[0].size, nbytes(*terms), terms[0].size),
    )(*terms)


def lane_blocks(pairs):
    return [(pair, side) for pair in range(pairs) for side in range(2)]


def gather_first_kernel(near, far, other_near, other_far, out):
    residues = near.shape[1]
    lanes = 2 * HEAD_DIM
    for n, (pair, side) in enumerate(lane_blocks(near.shape[2] // lanes)):
        at = slice(pair * lanes, (pair + 1) * lanes)
        out[:, :residues, n * lanes : (n + 1) * lanes] = (near, far)[side][:, :, at]
        out[:, residues:, n * lanes : (n + 1) * lanes] = (other_near, other_far)[side][:, :, at]


def gather_first(values, others):
    heads, residues, depth = values[0].shape
    return pl.pallas_call(
        gather_first_kernel,
        out_shape=jax.ShapeDtypeStruct((heads, 2 * residues, 2 * depth), BF16),
        compiler_params=params(),
        cost_estimate=cost(0, 4 * nbytes(*values)),
    )(*values, *others)


def gather_kernel(count, place, *refs):
    out = refs[-1]
    rows = refs[0].shape[1]
    for n, ref in enumerate(refs[:-1]):
        start = (n // count) * count * rows + jnp.bitwise_xor(place[3], n % count) * rows
        out[:, pl.ds(pl.multiple_of(start, rows), rows), :] = ref[...]


def gather(place, values, others):
    heads, rows, depth = values[0].shape
    count = len(values)
    return pl.pallas_call(
        functools.partial(gather_kernel, count),
        in_specs=[SMEM] + [FULL] * (2 * count),
        out_specs=FULL,
        out_shape=jax.ShapeDtypeStruct((heads, 2 * count * rows, depth), BF16),
        compiler_params=params(),
        cost_estimate=cost(0, 4 * nbytes(*values)),
    )(place, *values, *others)


def value_kernel(count, place, *refs):
    pieces, values, outs, hold = refs[:count], refs[count], refs[count + 1 : -1], refs[-1]
    heads, rows = pieces[0].shape[0], pieces[0].shape[1]
    lanes = 2 * HEAD_DIM
    for head in range(heads):
        if count == 1:
            weights = pieces[0][head]
        else:
            for e, piece in enumerate(pieces):
                start = pl.multiple_of(jnp.bitwise_xor(place[4], e) * rows, rows)
                hold[pl.ds(start, rows), :] = piece[head].astype(hold.dtype)
            weights = hold[...].astype(BF16)
        made = dot(weights, values[head]).astype(BF16)
        for n, (pair, side) in enumerate(lane_blocks(made.shape[1] // (2 * lanes))):
            outs[side][head, :, pair * lanes : (pair + 1) * lanes] = made[:, n * lanes : (n + 1) * lanes]


def weighted_values(place, pieces, values):
    heads, rows, residues = pieces[0].shape
    depth = values.shape[2]
    rows *= len(pieces)
    return pl.pallas_call(
        functools.partial(value_kernel, len(pieces)),
        in_specs=[SMEM] + [FULL] * (len(pieces) + 1),
        out_specs=[FULL] * 2,
        out_shape=[jax.ShapeDtypeStruct((heads, rows, depth // 2), BF16)] * 2,
        scratch_shapes=[pltpu.VMEM((rows, residues), hold_type(pieces[0].shape[1]))],
        compiler_params=params(),
        cost_estimate=cost(2 * heads * rows * residues * depth, nbytes(*pieces, values)),
    )(place, *pieces, values)


def normalized(rows, x, out_weight, gain):
    summed = x.astype(F32) + dot(rows, out_weight[...])
    mean_sq = jnp.mean(summed * summed, axis=-1, keepdims=True)
    return summed * lax.rsqrt(mean_sq + epsilon) * gain[...].astype(F32)


def head_columns(refs, lane):
    return jnp.concatenate(
        [ref[head][:, lane : lane + HEAD_DIM] for ref in refs for head in range(ref.shape[0])],
        axis=1,
    )


def next_kernel(g, place, *refs):
    attended_refs, (near, far, out_weight, gain), weights, outs = refs[:8], refs[8:12], refs[12:15], refs[15:]
    streams, projections = outs[:-3], outs[-3:]
    rows, depth = attended_refs[0].shape[1:]
    parts = [(side, s) for side in range(2) for s in range(2)]
    start = 0
    if near.shape[1] != rows:
        start = pl.multiple_of(jnp.bitwise_xor(place[3], g) * rows, rows)
    for p in range(depth // (2 * HEAD_DIM)):
        attended = [
            head_columns(attended_refs[4 * side : 4 * side + 4], (2 * p + s) * HEAD_DIM) for side, s in parts
        ]
        x = jnp.concatenate(
            [(near, far)[side][2 * p + s, pl.ds(start, rows), :] for side, s in parts], axis=0
        )
        made = normalized(jnp.concatenate(attended, axis=0), x, out_weight, gain).astype(BF16)
        for n, (side, s) in enumerate(parts):
            if side < len(streams):
                streams[side][2 * p + s] = made[n * rows : (n + 1) * rows]
        store_projections(made, weights, len(parts), p * len(parts) * HEAD_DIM, projections)


def next_layer(place, g, attended, near, far, out_weight, gain, weights, both):
    seqs, _, width = near.shape
    heads, rows, depth = attended[0].shape
    depth *= 2
    streams = 2 if both else 1
    flops = 4 * seqs * rows * width * (3 * weights[0].shape[1] + width)
    return pl.pallas_call(
        functools.partial(next_kernel, g),
        in_specs=[SMEM] + [FULL] * 15,
        out_specs=[FULL] * (streams + 3),
        out_shape=[jax.ShapeDtypeStruct((seqs, rows, width), BF16)] * streams
        + [jax.ShapeDtypeStruct((heads, rows, depth), BF16)] * 3,
        compiler_params=params(),
        cost_estimate=cost(flops, 8 * seqs * rows * width + nbytes(out_weight, *weights)),
    )(place, *attended, near, far, out_weight, gain, *weights)


def last_kernel(place, a0, a1, a2, a3, x, out_weight, gain, keep, send):
    x_bit, core = place[0], place[1]
    seqs, rows, _ = x.shape
    quarter = keep.shape[2]
    columns = [head_columns((a0, a1, a2, a3), s * HEAD_DIM) for s in range(seqs)]
    old = jnp.concatenate([x[s] for s in range(seqs)], axis=0)
    made = normalized(jnp.concatenate(columns, axis=0), old, out_weight, gain)
    half = jnp.where(x_bit == 1, made[:, 2 * quarter :], made[:, : 2 * quarter])
    low, high = half[:, :quarter], half[:, quarter:]
    mine, theirs = jnp.where(core == 1, high, low), jnp.where(core == 1, low, high)
    for s in range(seqs):
        keep[s % 2, s // 2] = mine[s * rows : (s + 1) * rows].T.astype(BF16)
        send[s % 2, s // 2] = theirs[s * rows : (s + 1) * rows].T.astype(BF16)


def last_layer(place, attended, x, out_weight, gain):
    seqs, rows, width = x.shape
    made = pl.pallas_call(
        last_kernel,
        in_specs=[SMEM] + [FULL] * 7,
        out_specs=[FULL] * 2,
        out_shape=[jax.ShapeDtypeStruct((2, seqs // 2, width // 4, rows), BF16)] * 2,
        compiler_params=params(),
        cost_estimate=cost(2 * seqs * rows * width * width, 3 * nbytes(x) + nbytes(out_weight)),
    )(place, *attended, x, out_weight, gain)
    return [a.reshape(seqs, width // 4, rows) for a in made]


def placed_kernel(count, place, *refs):
    out = refs[-1]
    rows = refs[0].shape[2]
    for n, ref in enumerate(refs[:-1]):
        core = jnp.bitwise_xor(place[1], n // count)
        start = (core * count + jnp.bitwise_xor(place[3], n % count)) * rows
        out[:, :, pl.ds(pl.multiple_of(start, rows), rows)] = ref[...]


def placed(place, kept, other):
    seqs, width, rows = kept[0].shape
    count = len(kept)
    return pl.pallas_call(
        functools.partial(placed_kernel, count),
        in_specs=[SMEM] + [FULL] * (2 * count),
        out_specs=FULL,
        out_shape=jax.ShapeDtypeStruct((seqs, width, 2 * count * rows), BF16),
        compiler_params=params(),
        cost_estimate=cost(0, 4 * nbytes(*kept)),
    )(place, *kept, *other)


def on_device(tokens, qkv_weight, out_weight, norm_gain):
    seqs, residues, _ = tokens.shape
    layers, width = norm_gain.shape
    n_rows, n_groups = lax.axis_size("rows"), lax.axis_size("heads")
    all_heads = width // HEAD_DIM
    row, group = lax.axis_index("rows"), lax.axis_index("heads")
    core, x_bit = group % 2, group // 2
    y_bit, z = row % 2, row // 2
    depth = n_rows // 2
    own = x_bit * 2 + y_bit
    heads = all_heads // 4
    own_width = heads * HEAD_DIM
    half = residues // 2
    scale = 1.0 / (HEAD_DIM * seqs * n_rows) ** 0.5
    count = min(depth, PIECES)
    each = depth // count
    place = jnp.stack([x_bit, core, z, z // each, z % each]).astype(jnp.int32)

    def over_core(a):
        return lax.ppermute(a, "heads", [(i, i ^ 1) for i in range(n_groups)])

    def over_x(a):
        return lax.ppermute(a, "heads", [(i, i ^ 2) for i in range(n_groups)])

    def over_y(a):
        return lax.ppermute(a, "rows", [(i, i ^ 1) for i in range(n_rows)])

    def over_xy(a):
        order = [(r * n_groups + g, (r ^ 1) * n_groups + (g ^ 2)) for r in range(n_rows) for g in range(n_groups)]
        return lax.ppermute(a, ("rows", "heads"), order)

    def over_z(a, d):
        return lax.ppermute(a, "rows", [(i, i ^ (2 * d)) for i in range(n_rows)])

    def own_columns(layer, at):
        return tuple(
            lax.dynamic_slice(
                qkv_weight, (layer, 0, which, at * own_width), (1, width, 1, own_width)
            ).reshape(width, own_width)
            for which in range(qkv_weight.shape[2])
        )

    def out_rows(layer, at):
        parts = [
            lax.dynamic_slice(out_weight, (layer, (at ^ d) * own_width, 0), (1, own_width, width))[0]
            for d in (0, 2, 1, 3)
        ]
        return jnp.concatenate(parts, axis=0)

    def packed(which):
        part = lax.dynamic_slice_in_dim(tokens, which * half, half, 1)
        return jnp.concatenate([part[: seqs // 2], part[seqs // 2 :]], axis=2)

    mine = packed(core)
    sibling = over_core(packed(1 - core))
    x_mine, y_mine = over_x(mine), over_y(mine)
    x_sibling, y_sibling = over_x(sibling), over_y(sibling)
    d_mine, d_sibling = over_y(x_mine), over_x(y_sibling)
    weight = own_columns(0, own)
    streams, queries, keys, values = [], [], [], []
    for pieces in ((mine, sibling, x_mine, x_sibling), (y_mine, y_sibling, d_mine, d_sibling)):
        made = first(place, pieces, weight, heads)
        for kept, one in zip((streams, queries, keys, values), made):
            kept.append(one)
    near, far = [streams[0]] * count, [streams[1]] * count

    for layer in range(layers):
        more = layer + 1 < layers
        other_keys = [over_core(k) for k in keys]
        other_values = [over_core(v) for v in values]
        if layer == 0:
            chunks = score_chunks(place, queries, keys, other_keys, scale, depth)
        else:
            chunks = joined_score_chunks(place, queries, keys, other_keys, scale, depth)
        terms = [chunks[0]] + [over_z(chunks[d], d) for d in range(1, depth)]
        if layer == 0:
            value = gather_first(values, other_values)
        else:
            value = gather(place, values, other_values)
        own_late, kept = lax.optimization_barrier((own, chunks[0]))
        out_mat = out_rows(layer, own_late)
        weight = own_columns(layer + 1, own_late) if more else ()
        terms[0], out_mat, weight, value = lax.optimization_barrier((kept, out_mat, weight, value))
        weights = softmax_sum(terms)
        gain = norm_gain[layer : layer + 1]
        pieces = [weights] + [over_z(weights, d) for d in range(1, depth)]
        attended, made = [], []
        both = layer + 2 < layers
        for g in range(count):
            near_part, far_part = weighted_values(place, pieces[g * each : (g + 1) * each], value)
            if g:
                before = attended[-1]
                near_part, far_part, before[1], before[2] = lax.optimization_barrier(
                    (near_part, far_part, before[1], before[2])
                )
            x_near, y_near = over_x(near_part), over_y(far_part)
            if not more:
                attended.append([near_part, x_near, y_near, over_xy(far_part)])
                continue
            x_far, y_far = over_x(far_part), over_y(near_part)
            if g:
                done = next_layer(place, g - 1, attended[-1], near[g - 1], far[g - 1], out_mat, gain, weight, both)
                x_near, y_near, *done = lax.optimization_barrier((x_near, y_near, *done))
                made.append(done)
            attended.append(
                [near_part, x_near, y_near, over_x(y_near), far_part, x_far, y_far, over_y(x_near)]
            )
        if more:
            g = count - 1
            made.append(
                next_layer(place, g, attended[g], near[g], far[g], out_mat, gain, weight, both)
            )
            near = [m[0] for m in made]
            far = [m[1] for m in made] if both else near
            queries, keys, values = ([m[i] for m in made] for i in (-3, -2, -1))
    kept, other = [], []
    for g in range(count):
        keep, send = last_layer(place, attended[g], near[g], out_mat, gain)
        kept.append(keep)
        other.append(over_core(send))
    return jnp.swapaxes(placed(place, kept, other), 1, 2)


def solution(mesh):
    return jax.shard_map(
        on_device,
        mesh=mesh,
        in_specs=(P("rows", None, "heads"), P(), P(), P()),
        out_specs=P("rows", None, "heads"),
        check_vma=False,
    )
```

```python
import functools

import jax
import jax.numpy as jnp
from jax import lax
from jax.experimental import pallas as pl
from jax.experimental.pallas import tpu as pltpu
from jax.sharding import PartitionSpec as P

HEAD_DIM = 64
epsilon = 1e-06
VMEM_LIMIT = 12 * 1024 * 1024
PIECES = 2
F32 = jnp.float32
BF16 = jnp.bfloat16


def dot(a, b):
    return jnp.dot(a, b, preferred_element_type=F32)


def dot_t(a, b):
    return lax.dot_general(a, b, (((1,), (1,)), ((), ())), preferred_element_type=F32)


def params():
    return pltpu.CompilerParams(vmem_limit_bytes=VMEM_LIMIT)


def cost(flops, nbytes, trans=0):
    return pl.CostEstimate(flops=int(flops), bytes_accessed=int(nbytes), transcendentals=int(trans))


def nbytes(*arrays):
    return sum(a.size * a.dtype.itemsize for a in arrays)


def hold_type(rows):
    return BF16 if rows % 16 == 0 else F32


SMEM = pl.BlockSpec(memory_space=pltpu.SMEM)


FULL = pl.BlockSpec(memory_space=pltpu.VMEM)


def store_projections(rows, weights, parts, lane, outs):
    count = rows.shape[0] // parts
    for weight, out in zip(weights, outs):
        projected = dot(rows, weight[...]).astype(BF16)
        for head in range(out.shape[0]):
            at = head * HEAD_DIM
            out[head, :, lane : lane + parts * HEAD_DIM] = jnp.concatenate(
                [projected[n * count : (n + 1) * count, at : at + HEAD_DIM] for n in range(parts)], axis=1
            )


def first_kernel(place, p0, p1, p2, p3, *refs):
    weights, x_out, outs = refs[:3], refs[3], refs[4:]
    x_bit, core = place[0], place[1]
    quarter = p0.shape[2] // 2
    for p in range(p0.shape[0]):
        pair = []
        for s in range(2):
            parts = [ref[p][:, s * quarter : (s + 1) * quarter] for ref in (p0, p1, p2, p3)]
            swapped = [jnp.where(core == 1, parts[t ^ 1], parts[t]) for t in range(4)]
            rows = jnp.concatenate(
                [jnp.where(x_bit == 1, swapped[t ^ 2], swapped[t]) for t in range(4)], axis=1
            )
            x_out[2 * p + s] = rows
            pair.append(rows)
        store_projections(jnp.concatenate(pair, axis=0), weights, 2, 2 * p * HEAD_DIM, outs)


def first(place, pieces, weights, heads):
    pairs, residues, half = pieces[0].shape
    width = 2 * half
    wide = jax.ShapeDtypeStruct((heads, residues, 2 * pairs * HEAD_DIM), BF16)
    flops = 12 * pairs * residues * width * weights[0].shape[1]
    return pl.pallas_call(
        first_kernel,
        in_specs=[SMEM] + [FULL] * 7,
        out_specs=[FULL] * 4,
        out_shape=[jax.ShapeDtypeStruct((2 * pairs, residues, width), BF16)] + [wide] * 3,
        compiler_params=params(),
        cost_estimate=cost(flops, 4 * nbytes(*pieces, *weights)),
    )(place, *pieces, *weights)


def score_kernel(scale, place, *refs):
    queries, keys, others, outs, hold = refs[0:2], refs[2:4], refs[4:6], refs[6:-1], refs[-1]
    z = place[2]
    heads, rows = outs[0].shape[0], outs[0].shape[1]
    residues = queries[0].shape[1]
    for head in range(heads):
        near = dot_t(queries[0][head], keys[0][head]) + dot_t(queries[1][head], keys[1][head])
        hold[:, :residues] = (near * scale).astype(hold.dtype)
        far = dot_t(queries[0][head], others[0][head]) + dot_t(queries[1][head], others[1][head])
        hold[:, residues:] = (far * scale).astype(hold.dtype)
        for d, out in enumerate(outs):
            start = pl.multiple_of(jnp.bitwise_xor(z, d) * rows, rows)
            out[head] = hold[pl.ds(start, rows), :].astype(BF16)


def score_chunks(place, queries, keys, others, scale, chunks):
    heads, residues, depth = queries[0].shape
    rows = residues // chunks
    args = (*queries, *keys, *others)
    return pl.pallas_call(
        functools.partial(score_kernel, scale),
        in_specs=[SMEM] + [FULL] * 6,
        out_specs=[FULL] * chunks,
        out_shape=[jax.ShapeDtypeStruct((heads, rows, 2 * residues), BF16)] * chunks,
        scratch_shapes=[pltpu.VMEM((residues, 2 * residues), hold_type(rows))],
        compiler_params=params(),
        cost_estimate=cost(8 * heads * residues * residues * depth, 2 * nbytes(*args)),
    )(place, *args)


def joined_score_kernel(scale, count, place, *refs):
    queries, keys, others = (refs[i * count : (i + 1) * count] for i in range(3))
    outs, key_hold, hold = refs[3 * count : -2], refs[-2], refs[-1]
    high, low = place[3], place[4]
    heads, rows = outs[0].shape[0], outs[0].shape[1]
    piece_rows = queries[0].shape[1]
    each = piece_rows // rows
    residues = count * piece_rows
    for head in range(heads):
        for side, group in enumerate((keys, others)):
            for g, ref in enumerate(group):
                start = side * residues + jnp.bitwise_xor(high, g) * piece_rows
                key_hold[pl.ds(pl.multiple_of(start, piece_rows), piece_rows), :] = ref[head]
        query = jnp.concatenate([ref[head] for ref in queries], axis=0)
        scores = dot_t(query, key_hold[...]) * scale
        if each == 1:
            for g, out in enumerate(outs):
                out[head] = scores[g * rows : (g + 1) * rows].astype(BF16)
        else:
            hold[...] = scores.astype(hold.dtype)
            for d, out in enumerate(outs):
                start = (d // each) * piece_rows + jnp.bitwise_xor(low, d % each) * rows
                out[head] = hold[pl.ds(pl.multiple_of(start, rows), rows), :].astype(BF16)


def joined_score_chunks(place, queries, keys, others, scale, chunks):
    heads, piece_rows, depth = queries[0].shape
    count = len(queries)
    residues = count * piece_rows
    rows = residues // chunks
    args = (*queries, *keys, *others)
    return pl.pallas_call(
        functools.partial(joined_score_kernel, scale, count),
        in_specs=[SMEM] + [FULL] * len(args),
        out_specs=[FULL] * chunks,
        out_shape=[jax.ShapeDtypeStruct((heads, rows, 2 * residues), BF16)] * chunks,
        scratch_shapes=[
            pltpu.VMEM((2 * residues, depth), BF16),
            pltpu.VMEM((residues, 2 * residues), hold_type(rows)),
        ],
        compiler_params=params(),
        cost_estimate=cost(4 * heads * residues * residues * depth, 2 * nbytes(*args)),
    )(place, *args)


def softmax_kernel(*refs):
    terms, out = refs[:-1], refs[-1]
    total = terms[0][...].astype(F32)
    for term in terms[1:]:
        total = total + term[...].astype(F32)
    top = jnp.max(total, axis=-1, keepdims=True)
    grown = jnp.exp(total - top)
    out[...] = (grown / jnp.sum(grown, axis=-1, keepdims=True)).astype(BF16)


def softmax_sum(terms):
    return pl.pallas_call(
        softmax_kernel,
        out_shape=jax.ShapeDtypeStruct(terms[0].shape, BF16),
        compiler_params=params(),
        cost_estimate=cost(10 * terms[0].size, nbytes(*terms), terms[0].size),
    )(*terms)


def lane_blocks(pairs):
    return [(pair, side) for pair in range(pairs) for side in range(2)]


def gather_first_kernel(near, far, other_near, other_far, out):
    residues = near.shape[1]
    lanes = 2 * HEAD_DIM
    for n, (pair, side) in enumerate(lane_blocks(near.shape[2] // lanes)):
        at = slice(pair * lanes, (pair + 1) * lanes)
        out[:, :residues, n * lanes : (n + 1) * lanes] = (near, far)[side][:, :, at]
        out[:, residues:, n * lanes : (n + 1) * lanes] = (other_near, other_far)[side][:, :, at]


def gather_first(values, others):
    heads, residues, depth = values[0].shape
    return pl.pallas_call(
        gather_first_kernel,
        out_shape=jax.ShapeDtypeStruct((heads, 2 * residues, 2 * depth), BF16),
        compiler_params=params(),
        cost_estimate=cost(0, 4 * nbytes(*values)),
    )(*values, *others)


def gather_kernel(count, place, *refs):
    out = refs[-1]
    rows = refs[0].shape[1]
    for n, ref in enumerate(refs[:-1]):
        start = (n // count) * count * rows + jnp.bitwise_xor(place[3], n % count) * rows
        out[:, pl.ds(pl.multiple_of(start, rows), rows), :] = ref[...]


def gather(place, values, others):
    heads, rows, depth = values[0].shape
    count = len(values)
    return pl.pallas_call(
        functools.partial(gather_kernel, count),
        in_specs=[SMEM] + [FULL] * (2 * count),
        out_specs=FULL,
        out_shape=jax.ShapeDtypeStruct((heads, 2 * count * rows, depth), BF16),
        compiler_params=params(),
        cost_estimate=cost(0, 4 * nbytes(*values)),
    )(place, *values, *others)


def value_kernel(count, place, *refs):
    pieces, values, outs, hold = refs[:count], refs[count], refs[count + 1 : -1], refs[-1]
    heads, rows = pieces[0].shape[0], pieces[0].shape[1]
    lanes = 2 * HEAD_DIM
    for head in range(heads):
        if count == 1:
            weights = pieces[0][head]
        else:
            for e, piece in enumerate(pieces):
                start = pl.multiple_of(jnp.bitwise_xor(place[4], e) * rows, rows)
                hold[pl.ds(start, rows), :] = piece[head].astype(hold.dtype)
            weights = hold[...].astype(BF16)
        made = dot(weights, values[head]).astype(BF16)
        for n, (pair, side) in enumerate(lane_blocks(made.shape[1] // (2 * lanes))):
            outs[side][head, :, pair * lanes : (pair + 1) * lanes] = made[:, n * lanes : (n + 1) * lanes]


def weighted_values(place, pieces, values):
    heads, rows, residues = pieces[0].shape
    depth = values.shape[2]
    rows *= len(pieces)
    return pl.pallas_call(
        functools.partial(value_kernel, len(pieces)),
        in_specs=[SMEM] + [FULL] * (len(pieces) + 1),
        out_specs=[FULL] * 2,
        out_shape=[jax.ShapeDtypeStruct((heads, rows, depth // 2), BF16)] * 2,
        scratch_shapes=[pltpu.VMEM((rows, residues), hold_type(pieces[0].shape[1]))],
        compiler_params=params(),
        cost_estimate=cost(2 * heads * rows * residues * depth, nbytes(*pieces, values)),
    )(place, *pieces, values)


def normalized(rows, x, out_weight, gain):
    summed = x.astype(F32) + dot(rows, out_weight[...])
    mean_sq = jnp.mean(summed * summed, axis=-1, keepdims=True)
    return summed * lax.rsqrt(mean_sq + epsilon) * gain[...].astype(F32)


def head_columns(refs, lane):
    return jnp.concatenate(
        [ref[head][:, lane : lane + HEAD_DIM] for ref in refs for head in range(ref.shape[0])],
        axis=1,
    )


def next_kernel(g, place, *refs):
    attended_refs, (near, far, out_weight, gain), weights, outs = refs[:8], refs[8:12], refs[12:15], refs[15:]
    streams, projections = outs[:-3], outs[-3:]
    rows, depth = attended_refs[0].shape[1:]
    parts = [(side, s) for side in range(2) for s in range(2)]
    start = 0
    if near.shape[1] != rows:
        start = pl.multiple_of(jnp.bitwise_xor(place[3], g) * rows, rows)
    for p in range(depth // (2 * HEAD_DIM)):
        attended = [
            head_columns(attended_refs[4 * side : 4 * side + 4], (2 * p + s) * HEAD_DIM) for side, s in parts
        ]
        x = jnp.concatenate(
            [(near, far)[side][2 * p + s, pl.ds(start, rows), :] for side, s in parts], axis=0
        )
        made = normalized(jnp.concatenate(attended, axis=0), x, out_weight, gain).astype(BF16)
        for n, (side, s) in enumerate(parts):
            if side < len(streams):
                streams[side][2 * p + s] = made[n * rows : (n + 1) * rows]
        store_projections(made, weights, len(parts), p * len(parts) * HEAD_DIM, projections)


def next_layer(place, g, attended, near, far, out_weight, gain, weights, both):
    seqs, _, width = near.shape
    heads, rows, depth = attended[0].shape
    depth *= 2
    streams = 2 if both else 1
    flops = 4 * seqs * rows * width * (3 * weights[0].shape[1] + width)
    return pl.pallas_call(
        functools.partial(next_kernel, g),
        in_specs=[SMEM] + [FULL] * 15,
        out_specs=[FULL] * (streams + 3),
        out_shape=[jax.ShapeDtypeStruct((seqs, rows, width), BF16)] * streams
        + [jax.ShapeDtypeStruct((heads, rows, depth), BF16)] * 3,
        compiler_params=params(),
        cost_estimate=cost(flops, 8 * seqs * rows * width + nbytes(out_weight, *weights)),
    )(place, *attended, near, far, out_weight, gain, *weights)


def last_kernel(place, a0, a1, a2, a3, x, out_weight, gain, keep, send):
    x_bit, core = place[0], place[1]
    seqs, rows, _ = x.shape
    quarter = keep.shape[2]
    columns = [head_columns((a0, a1, a2, a3), s * HEAD_DIM) for s in range(seqs)]
    old = jnp.concatenate([x[s] for s in range(seqs)], axis=0)
    made = normalized(jnp.concatenate(columns, axis=0), old, out_weight, gain)
    half = jnp.where(x_bit == 1, made[:, 2 * quarter :], made[:, : 2 * quarter])
    low, high = half[:, :quarter], half[:, quarter:]
    mine, theirs = jnp.where(core == 1, high, low), jnp.where(core == 1, low, high)
    for s in range(seqs):
        keep[s % 2, s // 2] = mine[s * rows : (s + 1) * rows].T.astype(BF16)
        send[s % 2, s // 2] = theirs[s * rows : (s + 1) * rows].T.astype(BF16)


def last_layer(place, attended, x, out_weight, gain):
    seqs, rows, width = x.shape
    made = pl.pallas_call(
        last_kernel,
        in_specs=[SMEM] + [FULL] * 7,
        out_specs=[FULL] * 2,
        out_shape=[jax.ShapeDtypeStruct((2, seqs // 2, width // 4, rows), BF16)] * 2,
        compiler_params=params(),
        cost_estimate=cost(2 * seqs * rows * width * width, 3 * nbytes(x) + nbytes(out_weight)),
    )(place, *attended, x, out_weight, gain)
    return [a.reshape(seqs, width // 4, rows) for a in made]


def placed_kernel(count, place, *refs):
    out = refs[-1]
    rows = refs[0].shape[2]
    for n, ref in enumerate(refs[:-1]):
        core = jnp.bitwise_xor(place[1], n // count)
        start = (core * count + jnp.bitwise_xor(place[3], n % count)) * rows
        out[:, :, pl.ds(pl.multiple_of(start, rows), rows)] = ref[...]


def placed(place, kept, other):
    seqs, width, rows = kept[0].shape
    count = len(kept)
    return pl.pallas_call(
        functools.partial(placed_kernel, count),
        in_specs=[SMEM] + [FULL] * (2 * count),
        out_specs=FULL,
        out_shape=jax.ShapeDtypeStruct((seqs, width, 2 * count * rows), BF16),
        compiler_params=params(),
        cost_estimate=cost(0, 4 * nbytes(*kept)),
    )(place, *kept, *other)


def on_device(tokens, qkv_weight, out_weight, norm_gain):
    seqs, residues, _ = tokens.shape
    layers, width = norm_gain.shape
    n_rows, n_groups = lax.axis_size("rows"), lax.axis_size("heads")
    all_heads = width // HEAD_DIM
    row = lax.axis_index("rows").astype(jnp.uint32)
    group = lax.axis_index("heads").astype(jnp.uint32)
    core, x_bit = group & 1, group >> 1
    y_bit, z = row & 1, row >> 1
    depth = n_rows // 2
    own = x_bit * 2 + y_bit
    heads = all_heads // 4
    own_width = heads * HEAD_DIM
    half = residues // 2
    scale = 1.0 / (HEAD_DIM * seqs * n_rows) ** 0.5
    count = min(depth, PIECES)
    each = depth // count
    place = jnp.stack([x_bit, core, z, z // each, z % each]).astype(jnp.int32)
    at_mine, at_theirs = core * half, (1 - core) * half
    at_columns = own * own_width
    at_rows = [(own ^ d) * own_width for d in (0, 2, 1, 3)]
    place, at_mine, at_theirs, at_columns, at_rows = lax.optimization_barrier(
        (place, at_mine, at_theirs, at_columns, at_rows)
    )
    zero = jnp.uint32(0)

    def over_core(a):
        return lax.ppermute(a, "heads", [(i, i ^ 1) for i in range(n_groups)])

    def over_x(a):
        return lax.ppermute(a, "heads", [(i, i ^ 2) for i in range(n_groups)])

    def over_y(a):
        return lax.ppermute(a, "rows", [(i, i ^ 1) for i in range(n_rows)])

    def over_xy(a):
        order = [(r * n_groups + g, (r ^ 1) * n_groups + (g ^ 2)) for r in range(n_rows) for g in range(n_groups)]
        return lax.ppermute(a, ("rows", "heads"), order)

    def over_z(a, d):
        return lax.ppermute(a, "rows", [(i, i ^ (2 * d)) for i in range(n_rows)])

    def own_columns(layer, at):
        return tuple(
            lax.dynamic_slice(
                qkv_weight, (jnp.uint32(layer), zero, jnp.uint32(which), at), (1, width, 1, own_width)
            ).reshape(width, own_width)
            for which in range(qkv_weight.shape[2])
        )

    def out_rows(layer, starts):
        parts = [
            lax.dynamic_slice(out_weight, (jnp.uint32(layer), at, zero), (1, own_width, width))[0]
            for at in starts
        ]
        return jnp.concatenate(parts, axis=0)

    def packed(at):
        part = lax.dynamic_slice(tokens, (zero, at, zero), (seqs, half, tokens.shape[2]))
        return jnp.concatenate([part[: seqs // 2], part[seqs // 2 :]], axis=2)

    mine = packed(at_mine)
    sibling = over_core(packed(at_theirs))
    x_mine, y_mine = over_x(mine), over_y(mine)
    x_sibling, y_sibling = over_x(sibling), over_y(sibling)
    d_mine, d_sibling = over_y(x_mine), over_x(y_sibling)
    weight = own_columns(0, at_columns)
    streams, queries, keys, values = [], [], [], []
    for pieces in ((mine, sibling, x_mine, x_sibling), (y_mine, y_sibling, d_mine, d_sibling)):
        made = first(place, pieces, weight, heads)
        for kept, one in zip((streams, queries, keys, values), made):
            kept.append(one)
    near, far = [streams[0]] * count, [streams[1]] * count

    for layer in range(layers):
        more = layer + 1 < layers
        other_keys = [over_core(k) for k in keys]
        other_values = [over_core(v) for v in values]
        if layer == 0:
            chunks = score_chunks(place, queries, keys, other_keys, scale, depth)
        else:
            chunks = joined_score_chunks(place, queries, keys, other_keys, scale, depth)
        terms = [chunks[0]] + [over_z(chunks[d], d) for d in range(1, depth)]
        if layer == 0:
            value = gather_first(values, other_values)
        else:
            value = gather(place, values, other_values)
        columns_late, rows_late, kept = lax.optimization_barrier((at_columns, at_rows, chunks[0]))
        out_mat = out_rows(layer, rows_late)
        weight = own_columns(layer + 1, columns_late) if more else ()
        terms[0], out_mat, weight, value = lax.optimization_barrier((kept, out_mat, weight, value))
        weights = softmax_sum(terms)
        gain = norm_gain[layer : layer + 1]
        pieces = [weights] + [over_z(weights, d) for d in range(1, depth)]
        attended, made = [], []
        both = layer + 2 < layers
        for g in range(count):
            near_part, far_part = weighted_values(place, pieces[g * each : (g + 1) * each], value)
            if g:
                before = attended[-1]
                near_part, far_part, before[1], before[2] = lax.optimization_barrier(
                    (near_part, far_part, before[1], before[2])
                )
            x_near, y_near = over_x(near_part), over_y(far_part)
            if not more:
                attended.append([near_part, x_near, y_near, over_xy(far_part)])
                continue
            x_far, y_far = over_x(far_part), over_y(near_part)
            if g:
                done = next_layer(place, g - 1, attended[-1], near[g - 1], far[g - 1], out_mat, gain, weight, both)
                x_near, y_near, *done = lax.optimization_barrier((x_near, y_near, *done))
                made.append(done)
            attended.append(
                [near_part, x_near, y_near, over_x(y_near), far_part, x_far, y_far, over_y(x_near)]
            )
        if more:
            g = count - 1
            made.append(
                next_layer(place, g, attended[g], near[g], far[g], out_mat, gain, weight, both)
            )
            near = [m[0] for m in made]
            far = [m[1] for m in made] if both else near
            queries, keys, values = ([m[i] for m in made] for i in (-3, -2, -1))
    kept, other = [], []
    for g in range(count):
        keep, send = last_layer(place, attended[g], near[g], out_mat, gain)
        kept.append(keep)
        other.append(over_core(send))
    return jnp.swapaxes(placed(place, kept, other), 1, 2)


def solution(mesh):
    return jax.shard_map(
        on_device,
        mesh=mesh,
        in_specs=(P("rows", None, "heads"), P(), P(), P()),
        out_specs=P("rows", None, "heads"),
        check_vma=False,
    )
```

```python
import functools

import jax
import jax.numpy as jnp
from jax import lax
from jax.experimental import pallas as pl
from jax.experimental.pallas import tpu as pltpu
from jax.sharding import PartitionSpec as P

HEAD_DIM = 64
epsilon = 1e-06
VMEM_LIMIT = 12 * 1024 * 1024
PIECES = 2
F32 = jnp.float32
BF16 = jnp.bfloat16


def dot(a, b):
    return jnp.dot(a, b, preferred_element_type=F32)


def dot_t(a, b):
    return lax.dot_general(a, b, (((1,), (1,)), ((), ())), preferred_element_type=F32)


def params():
    return pltpu.CompilerParams(vmem_limit_bytes=VMEM_LIMIT)


def cost(flops, nbytes, trans=0):
    return pl.CostEstimate(flops=int(flops), bytes_accessed=int(nbytes), transcendentals=int(trans))


def nbytes(*arrays):
    return sum(a.size * a.dtype.itemsize for a in arrays)


def hold_type(rows):
    return BF16 if rows % 16 == 0 else F32


SMEM = pl.BlockSpec(memory_space=pltpu.SMEM)


FULL = pl.BlockSpec(memory_space=pltpu.VMEM)


def store_projections(rows, weights, parts, lane, outs):
    count = rows.shape[0] // parts
    for weight, out in zip(weights, outs):
        projected = dot(rows, weight[...]).astype(BF16)
        for head in range(out.shape[0]):
            at = head * HEAD_DIM
            out[head, :, lane : lane + parts * HEAD_DIM] = jnp.concatenate(
                [projected[n * count : (n + 1) * count, at : at + HEAD_DIM] for n in range(parts)], axis=1
            )


def first_kernel(place, p0, p1, p2, p3, *refs):
    weights, x_out, outs = refs[:3], refs[3], refs[4:]
    x_bit, core = place[0], place[1]
    quarter = p0.shape[2] // 2
    for p in range(p0.shape[0]):
        pair = []
        for s in range(2):
            parts = [ref[p][:, s * quarter : (s + 1) * quarter] for ref in (p0, p1, p2, p3)]
            swapped = [jnp.where(core == 1, parts[t ^ 1], parts[t]) for t in range(4)]
            rows = jnp.concatenate(
                [jnp.where(x_bit == 1, swapped[t ^ 2], swapped[t]) for t in range(4)], axis=1
            )
            x_out[2 * p + s] = rows
            pair.append(rows)
        store_projections(jnp.concatenate(pair, axis=0), weights, 2, 2 * p * HEAD_DIM, outs)


def first(place, pieces, weights, heads):
    pairs, residues, half = pieces[0].shape
    width = 2 * half
    wide = jax.ShapeDtypeStruct((heads, residues, 2 * pairs * HEAD_DIM), BF16)
    flops = 12 * pairs * residues * width * weights[0].shape[1]
    return pl.pallas_call(
        first_kernel,
        in_specs=[SMEM] + [FULL] * 7,
        out_specs=[FULL] * 4,
        out_shape=[jax.ShapeDtypeStruct((2 * pairs, residues, width), BF16)] + [wide] * 3,
        compiler_params=params(),
        cost_estimate=cost(flops, 4 * nbytes(*pieces, *weights)),
    )(place, *pieces, *weights)


def score_kernel(scale, place, *refs):
    queries, keys, others, outs, hold = refs[0:2], refs[2:4], refs[4:6], refs[6:-1], refs[-1]
    z = place[2]
    heads, rows = outs[0].shape[0], outs[0].shape[1]
    residues = queries[0].shape[1]
    for head in range(heads):
        near = dot_t(queries[0][head], keys[0][head]) + dot_t(queries[1][head], keys[1][head])
        hold[:, :residues] = (near * scale).astype(hold.dtype)
        far = dot_t(queries[0][head], others[0][head]) + dot_t(queries[1][head], others[1][head])
        hold[:, residues:] = (far * scale).astype(hold.dtype)
        for d, out in enumerate(outs):
            start = pl.multiple_of(jnp.bitwise_xor(z, d) * rows, rows)
            out[head] = hold[pl.ds(start, rows), :].astype(BF16)


def score_chunks(place, queries, keys, others, scale, chunks):
    heads, residues, depth = queries[0].shape
    rows = residues // chunks
    args = (*queries, *keys, *others)
    return pl.pallas_call(
        functools.partial(score_kernel, scale),
        in_specs=[SMEM] + [FULL] * 6,
        out_specs=[FULL] * chunks,
        out_shape=[jax.ShapeDtypeStruct((heads, rows, 2 * residues), BF16)] * chunks,
        scratch_shapes=[pltpu.VMEM((residues, 2 * residues), hold_type(rows))],
        compiler_params=params(),
        cost_estimate=cost(8 * heads * residues * residues * depth, 2 * nbytes(*args)),
    )(place, *args)


def joined_score_kernel(scale, count, place, *refs):
    queries, keys, others = (refs[i * count : (i + 1) * count] for i in range(3))
    outs, key_hold, hold = refs[3 * count : -2], refs[-2], refs[-1]
    high, low = place[3], place[4]
    heads, rows = outs[0].shape[0], outs[0].shape[1]
    piece_rows = queries[0].shape[1]
    each = piece_rows // rows
    residues = count * piece_rows
    for head in range(heads):
        for side, group in enumerate((keys, others)):
            for g, ref in enumerate(group):
                start = side * residues + jnp.bitwise_xor(high, g) * piece_rows
                key_hold[pl.ds(pl.multiple_of(start, piece_rows), piece_rows), :] = ref[head]
        query = jnp.concatenate([ref[head] for ref in queries], axis=0)
        scores = dot_t(query, key_hold[...]) * scale
        if each == 1:
            for g, out in enumerate(outs):
                out[head] = scores[g * rows : (g + 1) * rows].astype(BF16)
        else:
            hold[...] = scores.astype(hold.dtype)
            for d, out in enumerate(outs):
                start = (d // each) * piece_rows + jnp.bitwise_xor(low, d % each) * rows
                out[head] = hold[pl.ds(pl.multiple_of(start, rows), rows), :].astype(BF16)


def joined_score_chunks(place, queries, keys, others, scale, chunks):
    heads, piece_rows, depth = queries[0].shape
    count = len(queries)
    residues = count * piece_rows
    rows = residues // chunks
    args = (*queries, *keys, *others)
    return pl.pallas_call(
        functools.partial(joined_score_kernel, scale, count),
        in_specs=[SMEM] + [FULL] * len(args),
        out_specs=[FULL] * chunks,
        out_shape=[jax.ShapeDtypeStruct((heads, rows, 2 * residues), BF16)] * chunks,
        scratch_shapes=[
            pltpu.VMEM((2 * residues, depth), BF16),
            pltpu.VMEM((residues, 2 * residues), hold_type(rows)),
        ],
        compiler_params=params(),
        cost_estimate=cost(4 * heads * residues * residues * depth, 2 * nbytes(*args)),
    )(place, *args)


def softmax_kernel(*refs):
    terms, out = refs[:-1], refs[-1]
    total = terms[0][...].astype(F32)
    for term in terms[1:]:
        total = total + term[...].astype(F32)
    top = jnp.max(total, axis=-1, keepdims=True)
    grown = jnp.exp(total - top)
    out[...] = (grown / jnp.sum(grown, axis=-1, keepdims=True)).astype(BF16)


def softmax_sum(terms):
    return pl.pallas_call(
        softmax_kernel,
        out_shape=jax.ShapeDtypeStruct(terms[0].shape, BF16),
        compiler_params=params(),
        cost_estimate=cost(10 * terms[0].size, nbytes(*terms), terms[0].size),
    )(*terms)


def lane_blocks(pairs):
    return [(pair, side) for pair in range(pairs) for side in range(2)]


def gather_first_kernel(near, far, other_near, other_far, out):
    residues = near.shape[1]
    lanes = 2 * HEAD_DIM
    for n, (pair, side) in enumerate(lane_blocks(near.shape[2] // lanes)):
        at = slice(pair * lanes, (pair + 1) * lanes)
        out[:, :residues, n * lanes : (n + 1) * lanes] = (near, far)[side][:, :, at]
        out[:, residues:, n * lanes : (n + 1) * lanes] = (other_near, other_far)[side][:, :, at]


def gather_first(values, others):
    heads, residues, depth = values[0].shape
    return pl.pallas_call(
        gather_first_kernel,
        out_shape=jax.ShapeDtypeStruct((heads, 2 * residues, 2 * depth), BF16),
        compiler_params=params(),
        cost_estimate=cost(0, 4 * nbytes(*values)),
    )(*values, *others)


def gather_kernel(count, place, *refs):
    out = refs[-1]
    rows = refs[0].shape[1]
    for n, ref in enumerate(refs[:-1]):
        start = (n // count) * count * rows + jnp.bitwise_xor(place[3], n % count) * rows
        out[:, pl.ds(pl.multiple_of(start, rows), rows), :] = ref[...]


def gather(place, values, others):
    heads, rows, depth = values[0].shape
    count = len(values)
    return pl.pallas_call(
        functools.partial(gather_kernel, count),
        in_specs=[SMEM] + [FULL] * (2 * count),
        out_specs=FULL,
        out_shape=jax.ShapeDtypeStruct((heads, 2 * count * rows, depth), BF16),
        compiler_params=params(),
        cost_estimate=cost(0, 4 * nbytes(*values)),
    )(place, *values, *others)


def value_kernel(count, place, *refs):
    pieces, values, outs, hold = refs[:count], refs[count], refs[count + 1 : -1], refs[-1]
    heads, rows = pieces[0].shape[0], pieces[0].shape[1]
    lanes = 2 * HEAD_DIM
    for head in range(heads):
        if count == 1:
            weights = pieces[0][head]
        else:
            for e, piece in enumerate(pieces):
                start = pl.multiple_of(jnp.bitwise_xor(place[4], e) * rows, rows)
                hold[pl.ds(start, rows), :] = piece[head].astype(hold.dtype)
            weights = hold[...].astype(BF16)
        made = dot(weights, values[head]).astype(BF16)
        for n, (pair, side) in enumerate(lane_blocks(made.shape[1] // (2 * lanes))):
            outs[side][head, :, pair * lanes : (pair + 1) * lanes] = made[:, n * lanes : (n + 1) * lanes]


def weighted_values(place, pieces, values):
    heads, rows, residues = pieces[0].shape
    depth = values.shape[2]
    rows *= len(pieces)
    return pl.pallas_call(
        functools.partial(value_kernel, len(pieces)),
        in_specs=[SMEM] + [FULL] * (len(pieces) + 1),
        out_specs=[FULL] * 2,
        out_shape=[jax.ShapeDtypeStruct((heads, rows, depth // 2), BF16)] * 2,
        scratch_shapes=[pltpu.VMEM((rows, residues), hold_type(pieces[0].shape[1]))],
        compiler_params=params(),
        cost_estimate=cost(2 * heads * rows * residues * depth, nbytes(*pieces, values)),
    )(place, *pieces, values)


def normalized(rows, x, out_weight, gain):
    summed = x.astype(F32) + dot(rows, out_weight[...])
    mean_sq = jnp.mean(summed * summed, axis=-1, keepdims=True)
    return summed * lax.rsqrt(mean_sq + epsilon) * gain[...].astype(F32)


def head_columns(refs, lane):
    return jnp.concatenate(
        [ref[head][:, lane : lane + HEAD_DIM] for ref in refs for head in range(ref.shape[0])],
        axis=1,
    )


def next_kernel(g, place, *refs):
    attended_refs, (near, far, out_weight, gain), weights, outs = refs[:8], refs[8:12], refs[12:15], refs[15:]
    streams, projections = outs[:-3], outs[-3:]
    rows, depth = attended_refs[0].shape[1:]
    parts = [(side, s) for side in range(2) for s in range(2)]
    start = 0
    if near.shape[1] != rows:
        start = pl.multiple_of(jnp.bitwise_xor(place[3], g) * rows, rows)
    for p in range(depth // (2 * HEAD_DIM)):
        attended = [
            head_columns(attended_refs[4 * side : 4 * side + 4], (2 * p + s) * HEAD_DIM) for side, s in parts
        ]
        x = jnp.concatenate(
            [(near, far)[side][2 * p + s, pl.ds(start, rows), :] for side, s in parts], axis=0
        )
        made = normalized(jnp.concatenate(attended, axis=0), x, out_weight, gain).astype(BF16)
        for n, (side, s) in enumerate(parts):
            if side < len(streams):
                streams[side][2 * p + s] = made[n * rows : (n + 1) * rows]
        store_projections(made, weights, len(parts), p * len(parts) * HEAD_DIM, projections)


def next_layer(place, g, attended, near, far, out_weight, gain, weights, both):
    seqs, _, width = near.shape
    heads, rows, depth = attended[0].shape
    depth *= 2
    streams = 2 if both else 1
    flops = 4 * seqs * rows * width * (3 * weights[0].shape[1] + width)
    return pl.pallas_call(
        functools.partial(next_kernel, g),
        in_specs=[SMEM] + [FULL] * 15,
        out_specs=[FULL] * (streams + 3),
        out_shape=[jax.ShapeDtypeStruct((seqs, rows, width), BF16)] * streams
        + [jax.ShapeDtypeStruct((heads, rows, depth), BF16)] * 3,
        compiler_params=params(),
        cost_estimate=cost(flops, 8 * seqs * rows * width + nbytes(out_weight, *weights)),
    )(place, *attended, near, far, out_weight, gain, *weights)


def last_kernel(place, a0, a1, a2, a3, x, out_weight, gain, keep, send):
    x_bit, core = place[0], place[1]
    seqs, rows, _ = x.shape
    quarter = keep.shape[2]
    columns = [head_columns((a0, a1, a2, a3), s * HEAD_DIM) for s in range(seqs)]
    old = jnp.concatenate([x[s] for s in range(seqs)], axis=0)
    made = normalized(jnp.concatenate(columns, axis=0), old, out_weight, gain)
    half = jnp.where(x_bit == 1, made[:, 2 * quarter :], made[:, : 2 * quarter])
    for s in range(seqs):
        turned = half[s * rows : (s + 1) * rows].T.astype(BF16)
        low, high = turned[:quarter], turned[quarter:]
        keep[s % 2, s // 2] = jnp.where(core == 1, high, low)
        send[s % 2, s // 2] = jnp.where(core == 1, low, high)


def last_layer(place, attended, x, out_weight, gain):
    seqs, rows, width = x.shape
    made = pl.pallas_call(
        last_kernel,
        in_specs=[SMEM] + [FULL] * 7,
        out_specs=[FULL] * 2,
        out_shape=[jax.ShapeDtypeStruct((2, seqs // 2, width // 4, rows), BF16)] * 2,
        compiler_params=params(),
        cost_estimate=cost(2 * seqs * rows * width * width, 3 * nbytes(x) + nbytes(out_weight)),
    )(place, *attended, x, out_weight, gain)
    return [a.reshape(seqs, width // 4, rows) for a in made]


def placed_kernel(count, place, *refs):
    out = refs[-1]
    rows = refs[0].shape[2]
    for n, ref in enumerate(refs[:-1]):
        core = jnp.bitwise_xor(place[1], n // count)
        start = (core * count + jnp.bitwise_xor(place[3], n % count)) * rows
        out[:, :, pl.ds(pl.multiple_of(start, rows), rows)] = ref[...]


def placed(place, kept, other):
    seqs, width, rows = kept[0].shape
    count = len(kept)
    return pl.pallas_call(
        functools.partial(placed_kernel, count),
        in_specs=[SMEM] + [FULL] * (2 * count),
        out_specs=FULL,
        out_shape=jax.ShapeDtypeStruct((seqs, width, 2 * count * rows), BF16),
        compiler_params=params(),
        cost_estimate=cost(0, 4 * nbytes(*kept)),
    )(place, *kept, *other)


def on_device(tokens, qkv_weight, out_weight, norm_gain):
    seqs, residues, _ = tokens.shape
    layers, width = norm_gain.shape
    n_rows, n_groups = lax.axis_size("rows"), lax.axis_size("heads")
    all_heads = width // HEAD_DIM
    row = lax.axis_index("rows").astype(jnp.uint32)
    group = lax.axis_index("heads").astype(jnp.uint32)
    core, x_bit = group & 1, group >> 1
    y_bit, z = row & 1, row >> 1
    depth = n_rows // 2
    own = x_bit * 2 + y_bit
    heads = all_heads // 4
    own_width = heads * HEAD_DIM
    half = residues // 2
    scale = 1.0 / (HEAD_DIM * seqs * n_rows) ** 0.5
    count = min(depth, PIECES)
    each = depth // count
    place = jnp.stack([x_bit, core, z, z // each, z % each]).astype(jnp.int32)
    at_mine, at_theirs = core * half, (1 - core) * half
    at_columns = own * own_width
    at_rows = [(own ^ d) * own_width for d in (0, 2, 1, 3)]
    place, at_mine, at_theirs, at_columns, at_rows = lax.optimization_barrier(
        (place, at_mine, at_theirs, at_columns, at_rows)
    )
    zero = jnp.uint32(0)

    def over_core(a):
        return lax.ppermute(a, "heads", [(i, i ^ 1) for i in range(n_groups)])

    def over_x(a):
        return lax.ppermute(a, "heads", [(i, i ^ 2) for i in range(n_groups)])

    def over_y(a):
        return lax.ppermute(a, "rows", [(i, i ^ 1) for i in range(n_rows)])

    def over_xy(a):
        order = [(r * n_groups + g, (r ^ 1) * n_groups + (g ^ 2)) for r in range(n_rows) for g in range(n_groups)]
        return lax.ppermute(a, ("rows", "heads"), order)

    def over_z(a, d):
        return lax.ppermute(a, "rows", [(i, i ^ (2 * d)) for i in range(n_rows)])

    def own_columns(layer, at):
        return tuple(
            lax.dynamic_slice(
                qkv_weight, (jnp.uint32(layer), zero, jnp.uint32(which), at), (1, width, 1, own_width)
            ).reshape(width, own_width)
            for which in range(qkv_weight.shape[2])
        )

    def out_rows(layer, starts):
        parts = [
            lax.dynamic_slice(out_weight, (jnp.uint32(layer), at, zero), (1, own_width, width))[0]
            for at in starts
        ]
        return jnp.concatenate(parts, axis=0)

    def packed(at):
        part = lax.dynamic_slice(tokens, (zero, at, zero), (seqs, half, tokens.shape[2]))
        return jnp.concatenate([part[: seqs // 2], part[seqs // 2 :]], axis=2)

    mine = packed(at_mine)
    sibling = over_core(packed(at_theirs))
    x_mine, y_mine = over_x(mine), over_y(mine)
    x_sibling, y_sibling = over_x(sibling), over_y(sibling)
    d_mine, d_sibling = over_y(x_mine), over_x(y_sibling)
    weight = own_columns(0, at_columns)
    streams, queries, keys, values = [], [], [], []
    for pieces in ((mine, sibling, x_mine, x_sibling), (y_mine, y_sibling, d_mine, d_sibling)):
        made = first(place, pieces, weight, heads)
        for kept, one in zip((streams, queries, keys, values), made):
            kept.append(one)
    near, far = [streams[0]] * count, [streams[1]] * count

    for layer in range(layers):
        more = layer + 1 < layers
        other_keys = [over_core(k) for k in keys]
        other_values = [over_core(v) for v in values]
        if layer == 0:
            chunks = score_chunks(place, queries, keys, other_keys, scale, depth)
        else:
            chunks = joined_score_chunks(place, queries, keys, other_keys, scale, depth)
        terms = [chunks[0]] + [over_z(chunks[d], d) for d in range(1, depth)]
        if layer == 0:
            value = gather_first(values, other_values)
        else:
            value = gather(place, values, other_values)
        columns_late, rows_late, kept = lax.optimization_barrier((at_columns, at_rows, chunks[0]))
        out_mat = out_rows(layer, rows_late)
        weight = own_columns(layer + 1, columns_late) if more else ()
        terms[0], out_mat, weight, value = lax.optimization_barrier((kept, out_mat, weight, value))
        weights = softmax_sum(terms)
        gain = norm_gain[layer : layer + 1]
        pieces = [weights] + [over_z(weights, d) for d in range(1, depth)]
        attended, made = [], []
        both = layer + 2 < layers
        for g in range(count):
            near_part, far_part = weighted_values(place, pieces[g * each : (g + 1) * each], value)
            if g:
                before = attended[-1]
                near_part, far_part, before[1], before[2] = lax.optimization_barrier(
                    (near_part, far_part, before[1], before[2])
                )
            x_near, y_near = over_x(near_part), over_y(far_part)
            if not more:
                attended.append([near_part, x_near, y_near, over_xy(far_part)])
                continue
            near_send, far_send = near_part, far_part
            if g:
                tied = (5, 6)
                near_send, far_send, *now = lax.optimization_barrier(
                    (near_part, far_part, *(before[i] for i in tied))
                )
                for i, one in zip(tied, now):
                    before[i] = one
            x_far, y_far = over_x(far_send), over_y(near_send)
            if g:
                done = next_layer(place, g - 1, attended[-1], near[g - 1], far[g - 1], out_mat, gain, weight, both)
                x_near, y_near, *done = lax.optimization_barrier((x_near, y_near, *done))
                made.append(done)
            attended.append(
                [near_part, x_near, y_near, over_x(y_near), far_part, x_far, y_far, over_y(x_near)]
            )
        if more:
            g = count - 1
            made.append(
                next_layer(place, g, attended[g], near[g], far[g], out_mat, gain, weight, both)
            )
            near = [m[0] for m in made]
            far = [m[1] for m in made] if both else near
            queries, keys, values = ([m[i] for m in made] for i in (-3, -2, -1))
    kept, other = [], []
    for g in range(count):
        keep, send = last_layer(place, attended[g], near[g], out_mat, gain)
        kept.append(keep)
        other.append(over_core(send))
    return jnp.swapaxes(placed(place, kept, other), 1, 2)


def solution(mesh):
    return jax.shard_map(
        on_device,
        mesh=mesh,
        in_specs=(P("rows", None, "heads"), P(), P(), P()),
        out_specs=P("rows", None, "heads"),
        check_vma=False,
    )
```

```python
import functools

import jax
import jax.numpy as jnp
from jax import lax
from jax.experimental import pallas as pl
from jax.experimental.pallas import tpu as pltpu
from jax.sharding import PartitionSpec as P

HEAD_DIM = 64
epsilon = 1e-06
VMEM_LIMIT = 12 * 1024 * 1024
PIECES = 2
F32 = jnp.float32
BF16 = jnp.bfloat16


def dot(a, b):
    return jnp.dot(a, b, preferred_element_type=F32)


def dot_t(a, b):
    return lax.dot_general(a, b, (((1,), (1,)), ((), ())), preferred_element_type=F32)


def params():
    return pltpu.CompilerParams(vmem_limit_bytes=VMEM_LIMIT)


def cost(flops, nbytes, trans=0):
    return pl.CostEstimate(flops=int(flops), bytes_accessed=int(nbytes), transcendentals=int(trans))


def nbytes(*arrays):
    return sum(a.size * a.dtype.itemsize for a in arrays)


def hold_type(rows):
    return BF16 if rows % 16 == 0 else F32


SMEM = pl.BlockSpec(memory_space=pltpu.SMEM)


FULL = pl.BlockSpec(memory_space=pltpu.VMEM)


def store_projections(rows, weights, parts, lane, outs):
    count = rows.shape[0] // parts
    for weight, out in zip(weights, outs):
        projected = dot(rows, weight[...]).astype(BF16)
        for head in range(out.shape[0]):
            at = head * HEAD_DIM
            out[head, :, lane : lane + parts * HEAD_DIM] = jnp.concatenate(
                [projected[n * count : (n + 1) * count, at : at + HEAD_DIM] for n in range(parts)], axis=1
            )


def first_kernel(place, p0, p1, p2, p3, *refs):
    weights, x_out, outs = refs[:3], refs[3], refs[4:]
    x_bit, core = place[0], place[1]
    quarter = p0.shape[2] // 2
    for p in range(p0.shape[0]):
        pair = []
        for s in range(2):
            parts = [ref[p][:, s * quarter : (s + 1) * quarter] for ref in (p0, p1, p2, p3)]
            swapped = [jnp.where(core == 1, parts[t ^ 1], parts[t]) for t in range(4)]
            rows = jnp.concatenate(
                [jnp.where(x_bit == 1, swapped[t ^ 2], swapped[t]) for t in range(4)], axis=1
            )
            x_out[2 * p + s] = rows
            pair.append(rows)
        store_projections(jnp.concatenate(pair, axis=0), weights, 2, 2 * p * HEAD_DIM, outs)


def first(place, pieces, weights, heads):
    pairs, residues, half = pieces[0].shape
    width = 2 * half
    wide = jax.ShapeDtypeStruct((heads, residues, 2 * pairs * HEAD_DIM), BF16)
    flops = 12 * pairs * residues * width * weights[0].shape[1]
    return pl.pallas_call(
        first_kernel,
        in_specs=[SMEM] + [FULL] * 7,
        out_specs=[FULL] * 4,
        out_shape=[jax.ShapeDtypeStruct((2 * pairs, residues, width), BF16)] + [wide] * 3,
        compiler_params=params(),
        cost_estimate=cost(flops, 4 * nbytes(*pieces, *weights)),
    )(place, *pieces, *weights)


def score_kernel(scale, place, *refs):
    queries, keys, others, outs, hold = refs[0:2], refs[2:4], refs[4:6], refs[6:-1], refs[-1]
    z = place[2]
    heads, rows = outs[0].shape[0], outs[0].shape[1]
    residues = queries[0].shape[1]
    for head in range(heads):
        near = dot_t(queries[0][head], keys[0][head]) + dot_t(queries[1][head], keys[1][head])
        far = dot_t(queries[0][head], others[0][head]) + dot_t(queries[1][head], others[1][head])
        mean = (jnp.sum(near, axis=1, keepdims=True) + jnp.sum(far, axis=1, keepdims=True)) / (2 * residues)
        hold[:, :residues] = ((near - mean) * scale).astype(hold.dtype)
        hold[:, residues:] = ((far - mean) * scale).astype(hold.dtype)
        for d, out in enumerate(outs):
            start = pl.multiple_of(jnp.bitwise_xor(z, d) * rows, rows)
            out[head] = hold[pl.ds(start, rows), :].astype(BF16)


def score_chunks(place, queries, keys, others, scale, chunks):
    heads, residues, depth = queries[0].shape
    rows = residues // chunks
    args = (*queries, *keys, *others)
    return pl.pallas_call(
        functools.partial(score_kernel, scale),
        in_specs=[SMEM] + [FULL] * 6,
        out_specs=[FULL] * chunks,
        out_shape=[jax.ShapeDtypeStruct((heads, rows, 2 * residues), BF16)] * chunks,
        scratch_shapes=[pltpu.VMEM((residues, 2 * residues), hold_type(rows))],
        compiler_params=params(),
        cost_estimate=cost(8 * heads * residues * residues * depth, 2 * nbytes(*args)),
    )(place, *args)


def joined_score_kernel(scale, count, place, *refs):
    queries, keys, others = (refs[i * count : (i + 1) * count] for i in range(3))
    outs, key_hold, hold = refs[3 * count : -2], refs[-2], refs[-1]
    high, low = place[3], place[4]
    heads, rows = outs[0].shape[0], outs[0].shape[1]
    piece_rows = queries[0].shape[1]
    each = piece_rows // rows
    residues = count * piece_rows
    for head in range(heads):
        for side, group in enumerate((keys, others)):
            for g, ref in enumerate(group):
                start = side * residues + jnp.bitwise_xor(high, g) * piece_rows
                key_hold[pl.ds(pl.multiple_of(start, piece_rows), piece_rows), :] = ref[head]
        query = jnp.concatenate([ref[head] for ref in queries], axis=0)
        scores = dot_t(query, key_hold[...])
        scores = (scores - jnp.mean(scores, axis=1, keepdims=True)) * scale
        if each == 1:
            for g, out in enumerate(outs):
                out[head] = scores[g * rows : (g + 1) * rows].astype(BF16)
        else:
            hold[...] = scores.astype(hold.dtype)
            for d, out in enumerate(outs):
                start = (d // each) * piece_rows + jnp.bitwise_xor(low, d % each) * rows
                out[head] = hold[pl.ds(pl.multiple_of(start, rows), rows), :].astype(BF16)


def joined_score_chunks(place, queries, keys, others, scale, chunks):
    heads, piece_rows, depth = queries[0].shape
    count = len(queries)
    residues = count * piece_rows
    rows = residues // chunks
    args = (*queries, *keys, *others)
    return pl.pallas_call(
        functools.partial(joined_score_kernel, scale, count),
        in_specs=[SMEM] + [FULL] * len(args),
        out_specs=[FULL] * chunks,
        out_shape=[jax.ShapeDtypeStruct((heads, rows, 2 * residues), BF16)] * chunks,
        scratch_shapes=[
            pltpu.VMEM((2 * residues, depth), BF16),
            pltpu.VMEM((residues, 2 * residues), hold_type(rows)),
        ],
        compiler_params=params(),
        cost_estimate=cost(4 * heads * residues * residues * depth, 2 * nbytes(*args)),
    )(place, *args)


def softmax_kernel(*refs):
    terms, out = refs[:-1], refs[-1]
    total = terms[0][...].astype(F32)
    for term in terms[1:]:
        total = total + term[...].astype(F32)
    top = jnp.max(total, axis=-1, keepdims=True)
    grown = jnp.exp(total - top)
    out[...] = (grown / jnp.sum(grown, axis=-1, keepdims=True)).astype(BF16)


def softmax_sum(terms):
    return pl.pallas_call(
        softmax_kernel,
        out_shape=jax.ShapeDtypeStruct(terms[0].shape, BF16),
        compiler_params=params(),
        cost_estimate=cost(10 * terms[0].size, nbytes(*terms), terms[0].size),
    )(*terms)


def lane_blocks(pairs):
    return [(pair, side) for pair in range(pairs) for side in range(2)]


def gather_first_kernel(near, far, other_near, other_far, out):
    residues = near.shape[1]
    lanes = 2 * HEAD_DIM
    for n, (pair, side) in enumerate(lane_blocks(near.shape[2] // lanes)):
        at = slice(pair * lanes, (pair + 1) * lanes)
        out[:, :residues, n * lanes : (n + 1) * lanes] = (near, far)[side][:, :, at]
        out[:, residues:, n * lanes : (n + 1) * lanes] = (other_near, other_far)[side][:, :, at]


def gather_first(values, others):
    heads, residues, depth = values[0].shape
    return pl.pallas_call(
        gather_first_kernel,
        out_shape=jax.ShapeDtypeStruct((heads, 2 * residues, 2 * depth), BF16),
        compiler_params=params(),
        cost_estimate=cost(0, 4 * nbytes(*values)),
    )(*values, *others)


def gather_kernel(count, place, *refs):
    out = refs[-1]
    rows = refs[0].shape[1]
    for n, ref in enumerate(refs[:-1]):
        start = (n // count) * count * rows + jnp.bitwise_xor(place[3], n % count) * rows
        out[:, pl.ds(pl.multiple_of(start, rows), rows), :] = ref[...]


def gather(place, values, others):
    heads, rows, depth = values[0].shape
    count = len(values)
    return pl.pallas_call(
        functools.partial(gather_kernel, count),
        in_specs=[SMEM] + [FULL] * (2 * count),
        out_specs=FULL,
        out_shape=jax.ShapeDtypeStruct((heads, 2 * count * rows, depth), BF16),
        compiler_params=params(),
        cost_estimate=cost(0, 4 * nbytes(*values)),
    )(place, *values, *others)


def value_kernel(count, place, *refs):
    pieces, values, outs, hold = refs[:count], refs[count], refs[count + 1 : -1], refs[-1]
    heads, rows = pieces[0].shape[0], pieces[0].shape[1]
    lanes = 2 * HEAD_DIM
    for head in range(heads):
        if count == 1:
            weights = pieces[0][head]
        else:
            for e, piece in enumerate(pieces):
                start = pl.multiple_of(jnp.bitwise_xor(place[4], e) * rows, rows)
                hold[pl.ds(start, rows), :] = piece[head].astype(hold.dtype)
            weights = hold[...].astype(BF16)
        made = dot(weights, values[head]).astype(BF16)
        for n, (pair, side) in enumerate(lane_blocks(made.shape[1] // (2 * lanes))):
            outs[side][head, :, pair * lanes : (pair + 1) * lanes] = made[:, n * lanes : (n + 1) * lanes]


def weighted_values(place, pieces, values):
    heads, rows, residues = pieces[0].shape
    depth = values.shape[2]
    rows *= len(pieces)
    return pl.pallas_call(
        functools.partial(value_kernel, len(pieces)),
        in_specs=[SMEM] + [FULL] * (len(pieces) + 1),
        out_specs=[FULL] * 2,
        out_shape=[jax.ShapeDtypeStruct((heads, rows, depth // 2), BF16)] * 2,
        scratch_shapes=[pltpu.VMEM((rows, residues), hold_type(pieces[0].shape[1]))],
        compiler_params=params(),
        cost_estimate=cost(2 * heads * rows * residues * depth, nbytes(*pieces, values)),
    )(place, *pieces, values)


def normalized(rows, x, out_weight, gain):
    summed = x.astype(F32) + dot(rows, out_weight[...])
    mean_sq = jnp.mean(summed * summed, axis=-1, keepdims=True)
    return summed * lax.rsqrt(mean_sq + epsilon) * gain[...].astype(F32)


def head_columns(refs, lane):
    return jnp.concatenate(
        [ref[head][:, lane : lane + HEAD_DIM] for ref in refs for head in range(ref.shape[0])],
        axis=1,
    )


def next_kernel(g, place, *refs):
    attended_refs, (near, far, out_weight, gain), weights, outs = refs[:8], refs[8:12], refs[12:15], refs[15:]
    streams, projections = outs[:-3], outs[-3:]
    rows, depth = attended_refs[0].shape[1:]
    parts = [(side, s) for side in range(2) for s in range(2)]
    start = 0
    if near.shape[1] != rows:
        start = pl.multiple_of(jnp.bitwise_xor(place[3], g) * rows, rows)
    for p in range(depth // (2 * HEAD_DIM)):
        attended = [
            head_columns(attended_refs[4 * side : 4 * side + 4], (2 * p + s) * HEAD_DIM) for side, s in parts
        ]
        x = jnp.concatenate(
            [(near, far)[side][2 * p + s, pl.ds(start, rows), :] for side, s in parts], axis=0
        )
        made = normalized(jnp.concatenate(attended, axis=0), x, out_weight, gain).astype(BF16)
        for n, (side, s) in enumerate(parts):
            if side < len(streams):
                streams[side][2 * p + s] = made[n * rows : (n + 1) * rows]
        store_projections(made, weights, len(parts), p * len(parts) * HEAD_DIM, projections)


def next_layer(place, g, attended, near, far, out_weight, gain, weights, both):
    seqs, _, width = near.shape
    heads, rows, depth = attended[0].shape
    depth *= 2
    streams = 2 if both else 1
    flops = 4 * seqs * rows * width * (3 * weights[0].shape[1] + width)
    return pl.pallas_call(
        functools.partial(next_kernel, g),
        in_specs=[SMEM] + [FULL] * 15,
        out_specs=[FULL] * (streams + 3),
        out_shape=[jax.ShapeDtypeStruct((seqs, rows, width), BF16)] * streams
        + [jax.ShapeDtypeStruct((heads, rows, depth), BF16)] * 3,
        compiler_params=params(),
        cost_estimate=cost(flops, 8 * seqs * rows * width + nbytes(out_weight, *weights)),
    )(place, *attended, near, far, out_weight, gain, *weights)


def last_kernel(place, a0, a1, a2, a3, x, out_weight, gain, keep, send):
    x_bit, core = place[0], place[1]
    seqs, rows, _ = x.shape
    quarter = keep.shape[2]
    columns = [head_columns((a0, a1, a2, a3), s * HEAD_DIM) for s in range(seqs)]
    old = jnp.concatenate([x[s] for s in range(seqs)], axis=0)
    made = normalized(jnp.concatenate(columns, axis=0), old, out_weight, gain)
    half = jnp.where(x_bit == 1, made[:, 2 * quarter :], made[:, : 2 * quarter])
    for s in range(seqs):
        turned = half[s * rows : (s + 1) * rows].T.astype(BF16)
        low, high = turned[:quarter], turned[quarter:]
        keep[s % 2, s // 2] = jnp.where(core == 1, high, low)
        send[s % 2, s // 2] = jnp.where(core == 1, low, high)


def last_layer(place, attended, x, out_weight, gain):
    seqs, rows, width = x.shape
    made = pl.pallas_call(
        last_kernel,
        in_specs=[SMEM] + [FULL] * 7,
        out_specs=[FULL] * 2,
        out_shape=[jax.ShapeDtypeStruct((2, seqs // 2, width // 4, rows), BF16)] * 2,
        compiler_params=params(),
        cost_estimate=cost(2 * seqs * rows * width * width, 3 * nbytes(x) + nbytes(out_weight)),
    )(place, *attended, x, out_weight, gain)
    return [a.reshape(seqs, width // 4, rows) for a in made]


def placed_kernel(count, place, *refs):
    out = refs[-1]
    rows = refs[0].shape[2]
    for n, ref in enumerate(refs[:-1]):
        core = jnp.bitwise_xor(place[1], n // count)
        start = (core * count + jnp.bitwise_xor(place[3], n % count)) * rows
        out[:, :, pl.ds(pl.multiple_of(start, rows), rows)] = ref[...]


def placed(place, kept, other):
    seqs, width, rows = kept[0].shape
    count = len(kept)
    return pl.pallas_call(
        functools.partial(placed_kernel, count),
        in_specs=[SMEM] + [FULL] * (2 * count),
        out_specs=FULL,
        out_shape=jax.ShapeDtypeStruct((seqs, width, 2 * count * rows), BF16),
        compiler_params=params(),
        cost_estimate=cost(0, 4 * nbytes(*kept)),
    )(place, *kept, *other)


def on_device(tokens, qkv_weight, out_weight, norm_gain):
    seqs, residues, _ = tokens.shape
    layers, width = norm_gain.shape
    n_rows, n_groups = lax.axis_size("rows"), lax.axis_size("heads")
    all_heads = width // HEAD_DIM
    row = lax.axis_index("rows").astype(jnp.uint32)
    group = lax.axis_index("heads").astype(jnp.uint32)
    core, x_bit = group & 1, group >> 1
    y_bit, z = row & 1, row >> 1
    depth = n_rows // 2
    own = x_bit * 2 + y_bit
    heads = all_heads // 4
    own_width = heads * HEAD_DIM
    half = residues // 2
    scale = 1.0 / (HEAD_DIM * seqs * n_rows) ** 0.5
    count = min(depth, PIECES)
    each = depth // count
    place = jnp.stack([x_bit, core, z, z // each, z % each]).astype(jnp.int32)
    at_mine, at_theirs = core * half, (1 - core) * half
    at_columns = own * own_width
    at_rows = [(own ^ d) * own_width for d in (0, 2, 1, 3)]
    place, at_mine, at_theirs, at_columns, at_rows = lax.optimization_barrier(
        (place, at_mine, at_theirs, at_columns, at_rows)
    )
    zero = jnp.uint32(0)

    def over_core(a):
        return lax.ppermute(a, "heads", [(i, i ^ 1) for i in range(n_groups)])

    def over_x(a):
        return lax.ppermute(a, "heads", [(i, i ^ 2) for i in range(n_groups)])

    def over_y(a):
        return lax.ppermute(a, "rows", [(i, i ^ 1) for i in range(n_rows)])

    def over_xy(a):
        order = [(r * n_groups + g, (r ^ 1) * n_groups + (g ^ 2)) for r in range(n_rows) for g in range(n_groups)]
        return lax.ppermute(a, ("rows", "heads"), order)

    def over_z(a, d):
        return lax.ppermute(a, "rows", [(i, i ^ (2 * d)) for i in range(n_rows)])

    def own_columns(layer, at):
        return tuple(
            lax.dynamic_slice(
                qkv_weight, (jnp.uint32(layer), zero, jnp.uint32(which), at), (1, width, 1, own_width)
            ).reshape(width, own_width)
            for which in range(qkv_weight.shape[2])
        )

    def out_rows(layer, starts):
        parts = [
            lax.dynamic_slice(out_weight, (jnp.uint32(layer), at, zero), (1, own_width, width))[0]
            for at in starts
        ]
        return jnp.concatenate(parts, axis=0)

    def packed(at):
        part = lax.dynamic_slice(tokens, (zero, at, zero), (seqs, half, tokens.shape[2]))
        return jnp.concatenate([part[: seqs // 2], part[seqs // 2 :]], axis=2)

    mine = packed(at_mine)
    sibling = over_core(packed(at_theirs))
    x_mine, y_mine = over_x(mine), over_y(mine)
    x_sibling, y_sibling = over_x(sibling), over_y(sibling)
    d_mine, d_sibling = over_y(x_mine), over_x(y_sibling)
    weight = own_columns(0, at_columns)
    streams, queries, keys, values = [], [], [], []
    for pieces in ((mine, sibling, x_mine, x_sibling), (y_mine, y_sibling, d_mine, d_sibling)):
        made = first(place, pieces, weight, heads)
        for kept, one in zip((streams, queries, keys, values), made):
            kept.append(one)
    near, far = [streams[0]] * count, [streams[1]] * count

    for layer in range(layers):
        more = layer + 1 < layers
        other_keys = [over_core(k) for k in keys]
        other_values = [over_core(v) for v in values]
        if layer == 0:
            chunks = score_chunks(place, queries, keys, other_keys, scale, depth)
        else:
            chunks = joined_score_chunks(place, queries, keys, other_keys, scale, depth)
        terms = [chunks[0]] + [over_z(chunks[d], d) for d in range(1, depth)]
        if layer == 0:
            value = gather_first(values, other_values)
        else:
            value = gather(place, values, other_values)
        columns_late, rows_late, kept = lax.optimization_barrier((at_columns, at_rows, chunks[0]))
        out_mat = out_rows(layer, rows_late)
        weight = own_columns(layer + 1, columns_late) if more else ()
        terms[0], out_mat, weight, value = lax.optimization_barrier((kept, out_mat, weight, value))
        weights = softmax_sum(terms)
        gain = norm_gain[layer : layer + 1]
        pieces = [weights] + [over_z(weights, d) for d in range(1, depth)]
        attended, made = [], []
        both = layer + 2 < layers
        for g in range(count):
            near_part, far_part = weighted_values(place, pieces[g * each : (g + 1) * each], value)
            if g:
                before = attended[-1]
                near_part, far_part, before[1], before[2] = lax.optimization_barrier(
                    (near_part, far_part, before[1], before[2])
                )
            x_near, y_near = over_x(near_part), over_y(far_part)
            if not more:
                attended.append([near_part, x_near, y_near, over_xy(far_part)])
                continue
            near_send, far_send = near_part, far_part
            if g:
                tied = (5, 6)
                near_send, far_send, *now = lax.optimization_barrier(
                    (near_part, far_part, *(before[i] for i in tied))
                )
                for i, one in zip(tied, now):
                    before[i] = one
            x_far, y_far = over_x(far_send), over_y(near_send)
            if g:
                done = next_layer(place, g - 1, attended[-1], near[g - 1], far[g - 1], out_mat, gain, weight, both)
                x_near, y_near, *done = lax.optimization_barrier((x_near, y_near, *done))
                made.append(done)
            attended.append(
                [near_part, x_near, y_near, over_x(y_near), far_part, x_far, y_far, over_y(x_near)]
            )
        if more:
            g = count - 1
            made.append(
                next_layer(place, g, attended[g], near[g], far[g], out_mat, gain, weight, both)
            )
            near = [m[0] for m in made]
            far = [m[1] for m in made] if both else near
            queries, keys, values = ([m[i] for m in made] for i in (-3, -2, -1))
    kept, other = [], []
    for g in range(count):
        keep, send = last_layer(place, attended[g], near[g], out_mat, gain)
        kept.append(keep)
        other.append(over_core(send))
    return jnp.swapaxes(placed(place, kept, other), 1, 2)


def solution(mesh):
    return jax.shard_map(
        on_device,
        mesh=mesh,
        in_specs=(P("rows", None, "heads"), P(), P(), P()),
        out_specs=P("rows", None, "heads"),
        check_vma=False,
    )
```
